512 devices in a mesh: section: 8 (over y, core), expert: 64 (over x, z).
Axes of the slice: x: 4, y: 4, z: 16, core: 2. Of those that a mesh axis runs over, the one named last changes fastest.
Arguments:
- x_fwd: bfloat16 [8, 6144, 3584], P('section', 'expert'), may hold values from -6 to 6
- ids_fwd: int32 [8, 6144, 8], P('section', 'expert'), may hold values from 0 to 255, as said below
- gates_fwd: float32 [8, 6144, 8], P('section', 'expert'), may hold values from 0.2 to 1
- dy_bwd: bfloat16 [8, 6144, 3584], P('section', 'expert'), may hold values from -6 to 6
- ids_bwd: int32 [8, 6144, 8], P('section', 'expert'), may hold values from 0 to 255, as said below
- gates_bwd: float32 [8, 6144, 8], P('section', 'expert'), may hold values from 0.2 to 1
- saved_hidden: float32 [8, 512, 8192], P('section', None, 'expert'), may hold values from -6 to 6
- w_up: bfloat16 [8, 3584, 8192], P('section', None, 'expert'), may hold values from -0.09375 to 0.09375
- w_down: bfloat16 [8, 8192, 3584], P('section', 'expert'), may hold values from -0.125 to 0.125
Outputs:
- next_fwd: bfloat16 [8, 6144, 3584], P('section', 'expert')
- next_bwd: bfloat16 [8, 6144, 3584], P('section', 'expert')
The draws below stay inside these ranges and needn't reach their ends.
Inputs may be any that keep to these rules, and one draw needn't show every extreme that they name: `ids_fwd`: each row names 8 different experts, at most one of them below 4. In the rows of one device at most 8 rows name any one expert below 4; in each layer one such expert is named by exactly 8 rows on every device. `ids_bwd`: as for ids_fwd.
All inputs are finite; a program needn't handle non-finite values.
Results may differ from the reference program's by a relative error of at most 0.0021.
Values may be sent and summed in bfloat16 or wider, within the bound.
A program may use at most 128 MiB of HBM per device.

```python
import math
import jax
import jax.numpy as jnp
from jax import lax

D = 3584
FF = 2048
EXPERTS = 256
TOPK = 8
FF_DEV = 128
CAP = 8
TOK_DEV = 96
SLICES = 16
EXP_WIN = 4
LAYERS = 8
TOKENS = 6144
N_EXPERT = 64


def route_ids(key):
    keys = jax.random.split(key, 5)
    hot_expert = jax.random.randint(keys[0], (LAYERS, 1, 1), 0, EXP_WIN)
    others = jax.random.randint(keys[1], (LAYERS, N_EXPERT, EXP_WIN), 1, 6)
    expert_iota = jnp.arange(EXP_WIN, dtype=jnp.int32)
    counts = jnp.where(expert_iota[None, None, :] == hot_expert, CAP, others)
    upper_end = jnp.cumsum(counts, axis=-1)
    starts = upper_end - counts
    token_iota = jnp.arange(TOK_DEV, dtype=jnp.int32)
    scores = jax.random.randint(keys[2], (LAYERS, N_EXPERT, TOK_DEV), 0, 2 ** 20) * TOK_DEV + token_iota
    token_rank = jnp.argsort(jnp.argsort(scores, axis=-1, stable=True), axis=-1, stable=True).astype(jnp.int32)
    inside = (token_rank[..., None] >= starts[:, :, None, :]) & (token_rank[..., None] < upper_end[:, :, None, :])
    routed = jnp.any(inside, axis=-1)
    chosen = jnp.sum(inside.astype(jnp.int32) * expert_iota, axis=-1)
    offset = jax.random.randint(keys[3], (LAYERS, N_EXPERT, TOK_DEV, 1), 0, EXPERTS - EXP_WIN)
    slot_iota = jnp.arange(TOPK, dtype=jnp.int32)
    other_ids = EXP_WIN + (offset + slot_iota) % (EXPERTS - EXP_WIN)
    window_slot = jax.random.randint(keys[4], (LAYERS, N_EXPERT, TOK_DEV, 1), 0, TOPK)
    ids = jnp.where(routed[..., None] & (slot_iota == window_slot), chosen[..., None], other_ids)
    return ids.reshape(LAYERS, N_EXPERT * TOK_DEV, TOPK).astype(jnp.int32)


def draw_ids_fwd(key, part):
    key = jax.random.fold_in(key, 11)
    return route_ids(key)


def draw_ids_bwd(key, part):
    key = jax.random.fold_in(key, 12)
    return route_ids(key)


def levels(key, extent, pieces, least, top_value):
    loudness = 1.0
    for dim, blocks in pieces:
        heights = jax.random.uniform(jax.random.fold_in(jax.random.fold_in(key, 6), dim), (blocks,), jnp.float32, least / len(pieces), top_value / len(pieces))
        loudness = loudness * jnp.repeat(jnp.exp(heights), extent[dim] // blocks).reshape((-1,) + (1,) * (len(extent) - 1 - dim))
    return loudness


def normal_values(stream_key, dims, width, reach, shards=(), held_as=jnp.bfloat16):
    array = width * jax.random.normal(stream_key, dims, jnp.float32)
    if shards:
        array = array * levels(stream_key, dims, shards, -0.22, 0.18)
    return jnp.clip(array, -reach, reach).astype(held_as)


def setup_inputs(seed: int = 0) -> dict:
    splits = jax.random.split(jax.random.key(seed), 10)
    x_fwd = normal_values(splits[0], (LAYERS, TOKENS, D), 1.0, 6.0, ((0, 8), (1, 64)))
    ids_fwd = draw_ids_fwd(jax.random.fold_in(splits[9], 71), 0)
    gates_fwd = jnp.clip(jnp.exp(math.log(1.0) - 1.609438 * jax.random.uniform(splits[2], (LAYERS, TOKENS, TOPK), jnp.float32) ** levels(splits[2], (LAYERS, TOKENS, TOPK), ((0, 8), (1, 64)), -0.2, 0.2)), 0.2, 1.0)
    dy_bwd = normal_values(splits[3], (LAYERS, TOKENS, D), 1.0, 6.0, ((0, 8), (1, 64)))
    ids_bwd = draw_ids_bwd(jax.random.fold_in(splits[9], 71), 0)
    gates_bwd = jnp.clip(jnp.exp(math.log(1.0) - 1.609438 * jax.random.uniform(splits[5], (LAYERS, TOKENS, TOPK), jnp.float32) ** levels(splits[5], (LAYERS, TOKENS, TOPK), ((0, 8), (1, 64)), -0.2, 0.2)), 0.2, 1.0)
    saved_hidden = normal_values(splits[6], (LAYERS, N_EXPERT * CAP, EXP_WIN * FF), 1.5, 6.0, ((0, 8), (2, 64)), jnp.float32)
    w_up = normal_values(splits[7], (LAYERS, D, EXP_WIN * FF), D ** -0.5, 0.09375, ((0, 8), (2, 64)))
    w_down = normal_values(splits[8], (LAYERS, EXP_WIN * FF, D), FF ** -0.5, 0.125, ((0, 8), (1, 64)))
    return {"x_fwd": x_fwd, "ids_fwd": ids_fwd, "gates_fwd": gates_fwd, "dy_bwd": dy_bwd, "ids_bwd": ids_bwd, "gates_bwd": gates_bwd, "saved_hidden": saved_hidden, "w_up": w_up, "w_down": w_down}


def routing(ids, gates):
    expert_iota = jnp.arange(EXP_WIN, dtype=jnp.int32)
    match = ids[:, :, None] == expert_iota[None, None, :]
    routed = jnp.any(match, axis=1).astype(jnp.int32)
    gate_each = jnp.sum(jnp.where(match, gates[:, :, None], jnp.float32(0.0)), axis=1)
    blocks = jnp.transpose(routed.reshape(N_EXPERT, TOK_DEV, EXP_WIN), (0, 2, 1))
    position = jnp.cumsum(blocks, axis=2) - blocks
    slot_iota = jnp.arange(CAP, dtype=jnp.int32)
    place = ((position[:, :, None, :] == slot_iota[None, None, :, None]) & (blocks[:, :, None, :] == 1)).astype(jnp.float32)
    gate_blocks = jnp.transpose(gate_each.reshape(N_EXPERT, TOK_DEV, EXP_WIN), (0, 2, 1))
    return place, gate_blocks


def slice_sums(values, weight):
    row_count = values.shape[0]
    lhs = values.astype(jnp.float32).reshape(row_count, SLICES, FF_DEV)
    rhs = weight.astype(jnp.float32).reshape(SLICES, FF_DEV, D)
    partial_value = jnp.einsum('rhf,hfd->hrd', lhs, rhs).astype(jnp.bfloat16)
    partial_value = lax.optimization_barrier(partial_value)
    return jnp.sum(partial_value.astype(jnp.float32), axis=0)


def gather_rows(place, tokens):
    blocks = tokens.reshape(N_EXPERT, TOK_DEV, D).astype(jnp.float32)
    return jnp.einsum('dect,dtf->edcf', place, blocks).astype(jnp.bfloat16)


def combine(tokens, place, gate_blocks, totals):
    weighting = place * gate_blocks[:, :, None, :]
    branch = jnp.einsum('dect,edcf->dtf', weighting, totals, precision=lax.Precision.HIGHEST)
    whole = tokens.reshape(N_EXPERT, TOK_DEV, D).astype(jnp.float32) + branch
    return whole.reshape(TOKENS, D).astype(jnp.bfloat16)


def layer_forward(tokens, ids, gates, w_up, w_down):
    place, gate_blocks = routing(ids, gates)
    rows = gather_rows(place, tokens)
    totals = []
    for index in range(EXP_WIN):
        flat_rows = rows[index].reshape(N_EXPERT * CAP, D)
        hidden = jnp.dot(flat_rows, w_up[:, index * FF:(index + 1) * FF], preferred_element_type=jnp.float32)
        activated = jax.nn.silu(hidden).astype(jnp.bfloat16)
        total = slice_sums(activated, w_down[index * FF:(index + 1) * FF])
        totals.append(total.reshape(N_EXPERT, CAP, D))
    return combine(tokens, place, gate_blocks, jnp.stack(totals))


def layer_backward(grads, ids, gates, saved, w_up, w_down):
    place, gate_blocks = routing(ids, gates)
    rows = gather_rows(place, grads)
    totals = []
    for index in range(EXP_WIN):
        flat_rows = rows[index].reshape(N_EXPERT * CAP, D)
        down_block = w_down[index * FF:(index + 1) * FF]
        grad_act = jnp.dot(flat_rows, down_block.T, preferred_element_type=jnp.float32)
        pre_act = saved[:, index * FF:(index + 1) * FF]
        sigmoid_h = jax.nn.sigmoid(pre_act)
        grad_hidden = (grad_act * sigmoid_h * (1.0 + pre_act * (1.0 - sigmoid_h))).astype(jnp.bfloat16)
        total = slice_sums(grad_hidden, w_up[:, index * FF:(index + 1) * FF].T)
        totals.append(total.reshape(N_EXPERT, CAP, D))
    return combine(grads, place, gate_blocks, jnp.stack(totals))


def reference(x_fwd, ids_fwd, gates_fwd, dy_bwd, ids_bwd, gates_bwd, saved_hidden, w_up, w_down):
    outputs = []
    inputs_grad = []
    for layer in range(LAYERS):
        outputs.append(layer_forward(x_fwd[layer], ids_fwd[layer], gates_fwd[layer], w_up[layer], w_down[layer]))
        inputs_grad.append(layer_backward(dy_bwd[layer], ids_bwd[layer], gates_bwd[layer], saved_hidden[layer], w_up[layer], w_down[layer]))
    next_fwd = jnp.roll(jnp.stack(outputs), 1, axis=0)
    next_bwd = jnp.roll(jnp.stack(inputs_grad), -1, axis=0)
    return next_fwd, next_bwd
```

```python
import functools

import jax
import jax.numpy as jnp
from jax import lax
from jax.experimental import pallas as pl
from jax.experimental.pallas import tpu as pltpu
from jax.sharding import PartitionSpec as P

MESH = pl.DeviceIdType.MESH
CAP = 8
SUB = 2 * CAP
FF = 2048
f32 = jnp.float32
bf16 = jnp.bfloat16


def tile_of(width):
    return 512 if width % 512 == 0 else 128


def routing(ids, gates, window):
    rows, choices = ids.shape
    span = SUB * window
    lane = lax.broadcasted_iota(jnp.int32, (rows, 2 * span), 1)
    expert = lax.div(lax.rem(lane, span), SUB)
    slot = lax.rem(lane, CAP)
    same_half = lax.div(lane, span) == lax.div(lax.rem(lane, SUB), CAP)
    routed = jnp.zeros((rows, 2 * span), f32)
    gate = jnp.zeros((rows, 2 * span), f32)
    for k in range(choices):
        match = ids[:, k : k + 1] == expert
        routed = jnp.where(match, 1.0, routed)
        gate = gate + jnp.where(match, gates[:, k : k + 1], 0.0)
    earlier = lax.broadcasted_iota(jnp.int32, (rows, rows), 1) < lax.broadcasted_iota(
        jnp.int32, (rows, rows), 0
    )
    position = jnp.dot(
        jnp.where(earlier, 1.0, 0.0).astype(bf16), routed.astype(bf16), preferred_element_type=f32
    )
    taken = (routed > 0.5) & (position == slot.astype(f32)) & same_half
    place = jnp.where(taken, 1.0, 0.0)
    return place, place * gate


def kernel(
    nsec, nx, nz,
    x_hbm, dy_hbm, idf_ref, gf_ref, idb_ref, gb_ref, saved_hbm, up_hbm, down_hbm,
    outf_hbm, outb_hbm,
    xin, rows, gall, gown, upw, downw, saved, ag, rs, stage, part, plr, near, near_plr, ysend, yrecv, obuf,
    load_sem, out_sem, xs_send, xs_recv, gs_send, gs_recv, ag_send, ag_recv, rs_send, rs_recv,
    near_send, near_recv, y_send, y_recv,
):
    half = nz // 2
    tokens, width = xin.shape[1], xin.shape[2]
    span = SUB * nx
    fold = width // 2
    hid = upw.shape[1] // 2
    tile = tile_of(width)
    ftile = tile_of(fold)
    early = range(nx // 2)
    late = range(nx // 2, nx)

    sec = lax.axis_index("section")
    me = lax.axis_index("expert")
    mx, mz = lax.div(me, nz), lax.rem(me, nz)
    right = (sec, mx * nz + lax.rem(mz + 1, nz))
    left = (sec, mx * nz + lax.rem(mz + nz - 1, nz))
    sec_up, sec_down = lax.rem(sec + 1, nsec), lax.rem(sec + nsec - 1, nsec)
    columns = [lax.rem(mx + i, nx) for i in range(nx)]
    targets = [lax.rem(mx + nx - i, nx) for i in range(nx)]
    out_way = (right, left)
    back_way = (left, right)

    def remote(src, dst, send, recv, device):
        return pltpu.make_async_remote_copy(
            src_ref=src, dst_ref=dst, send_sem=send, recv_sem=recv, device_id=device, device_id_type=MESH
        )

    def sub(i):
        return pl.ds(i * SUB, SUB)

    def sub_at(index):
        return pl.ds(pl.multiple_of(index * SUB, SUB), SUB)

    loads = [
        pltpu.make_async_copy(x_hbm, xin.at[0], load_sem.at[0]),
        pltpu.make_async_copy(dy_hbm, xin.at[1], load_sem.at[1]),
        pltpu.make_async_copy(up_hbm, upw.at[:, pl.ds(0, hid)], load_sem.at[2]),
        pltpu.make_async_copy(down_hbm, downw.at[pl.ds(0, hid)], load_sem.at[3]),
        pltpu.make_async_copy(saved_hbm, saved, load_sem.at[4]),
    ]
    for load in loads:
        load.start()

    peers = [right, left]
    peers += [(sec, columns[i] * nz + mz) for i in range(1, nx)]
    peers += [(s, columns[i] * nz + mz) for s in (sec_up, sec_down) for i in range(nx)]
    barrier = pltpu.get_barrier_semaphore()
    for peer in peers:
        pl.semaphore_signal(barrier, inc=1, device_id=peer, device_id_type=MESH)

    place_f, weight_f = routing(idf_ref[...], gf_ref[...], nx)
    place_b, weight_b = routing(idb_ref[...], gb_ref[...], nx)
    plr[0] = place_f.astype(bf16)
    plr[1] = place_b.astype(bf16)
    first = lax.broadcasted_iota(jnp.int32, place_f.shape, 1) < span
    chosen = jnp.where(first, place_f, place_b).T.astype(bf16)
    weight = jnp.sum(jnp.where(first, weight_f, weight_b).T, axis=1, keepdims=True)
    gall[...] = jnp.broadcast_to(weight[:span] + weight[span:], gall.shape)
    chosen_f, chosen_b = chosen[:span], chosen[span:]
    loads[0].wait()
    loads[1].wait()

    @pl.loop(0, width // tile)
    def _(step):
        cols = pl.ds(pl.multiple_of(step * tile, tile), tile)
        rows[:, cols] = (
            jnp.dot(chosen_f, xin[0, :, cols], preferred_element_type=f32)
            + jnp.dot(chosen_b, xin[1, :, cols], preferred_element_type=f32)
        ).astype(bf16)

    ag[0, 0, sub(0)] = rows[sub_at(mx)]
    gown[sub(0)] = gall[sub_at(mx)]
    pl.semaphore_wait(barrier, len(peers))

    def row_copy(i):
        device = (sec, targets[i] * nz + mz)
        return remote(
            rows.at[sub_at(targets[i])], ag.at[0, 0, sub(i)], xs_send.at[i - 1], xs_recv.at[i - 1], device
        )

    def gate_copy(i):
        device = (sec, targets[i] * nz + mz)
        return remote(
            gall.at[sub_at(targets[i])], gown.at[sub(i)], gs_send.at[i - 1], gs_recv.at[i - 1], device
        )

    def out_copy(s, d, i, own=False):
        src = ag.at[0, 0, sub(i)] if own else ag.at[s, d, sub(i)]
        send = ag_send.at[d] if own else ag_send.at[s + 1]
        return remote(src, ag.at[s + 1, d, sub(i)], send, ag_recv.at[s + 1, d, i], out_way[d])

    def far_copy(d, i):
        send = ag_send.at[half if d == 0 else half + 1]
        return remote(ag.at[half - 1, d, sub(i)], ag.at[0, 1, sub(i)], send, ag_recv.at[0, 1, i], out_way[d])

    for i in range(1, nx):
        row_copy(i).start()
    for d in range(2):
        out_copy(0, d, 0, own=True).start()
    for i in range(1, nx):
        gate_copy(i).start()

    next_of = ((sec_up, me), (sec_down, me))
    near_copies = [
        remote(src.at[h], dst.at[h], near_send.at[h, k], near_recv.at[h, k], next_of[h])
        for h in range(2)
        for k, (src, dst) in enumerate(((xin, near), (plr, near_plr)))
    ]
    for copy in near_copies:
        copy.start()

    for i in range(1, nx):
        row_copy(i).wait_recv()
        for d in range(2):
            out_copy(0, d, i, own=True).start()

    loads[2].wait()
    loads[3].wait()
    loads[4].wait()

    @pl.loop(0, width // tile)
    def _(step):
        cols = pl.ds(pl.multiple_of(step * tile, tile), tile)
        upw[cols, pl.ds(hid, hid)] = downw[pl.ds(0, hid), cols].T
        downw[pl.ds(hid, hid), cols] = upw[cols, pl.ds(0, hid)].T

    @pl.loop(0, nx)
    def _(column):
        value = saved[column]
        sig = jax.nn.sigmoid(value)
        saved[column] = sig * (1.0 + value * (1.0 - sig))

    def compute(s, sources):
        def add_up(step, total):
            cols = pl.ds(pl.multiple_of(step * tile, tile), tile)
            block = ag[s, :, :, cols].reshape(2 * span, tile)
            return total + jnp.dot(block, upw[cols, :], preferred_element_type=f32)

        total = lax.fori_loop(0, width // tile, add_up, jnp.zeros((2 * span, 2 * hid), f32))
        total = total.reshape(2 * nx, 2, CAP, 2 * hid)
        forward = total[:, 0, :, :hid]
        forward = forward * jax.nn.sigmoid(forward)
        slope = jnp.stack([saved[columns[i], source] for source in sources for i in range(nx)])
        backward = total[:, 1, :, hid:] * slope
        none = jnp.zeros_like(forward)
        inner = jnp.stack(
            [jnp.concatenate([forward, none], axis=-1), jnp.concatenate([none, backward], axis=-1)], axis=1
        )
        inner = inner.reshape(2 * span, 2 * hid).astype(bf16)

        @pl.loop(0, width // tile)
        def _(step):
            cols = pl.ds(pl.multiple_of(step * tile, tile), tile)
            result = jnp.dot(inner, downw[:, cols], preferred_element_type=f32)
            part[s, :, :, cols] = result.reshape(2, span, tile)

    def both(s):
        return (lax.rem(mz + nz - s, nz), lax.rem(mz + s, nz))

    @pl.loop(1, half - 1)
    def _(s):
        for i in range(nx):
            for d in range(2):
                out_copy(s - 1, d, i).wait_recv()
                out_copy(s, d, i).start()
        compute(s, both(s))

    for i in range(nx):
        for d in range(2):
            out_copy(half - 2, d, i).wait_recv()
            if i in (early, late)[d]:
                far_copy(d, i).start()
    compute(half - 1, both(half - 1))

    def back_copy(s, d, i):
        return remote(
            rs.at[s, d, sub(i)], rs.at[s - 1, d, sub(i)], rs_send.at[s], rs_recv.at[s - 1, d, i], back_way[d]
        )

    def first_copy(d, i):
        return remote(stage.at[sub(i)], rs.at[half - 1, d, sub(i)], rs_send.at[0], rs_recv.at[half - 1, d, i], back_way[d])

    for d in range(2):
        for i in (late, early)[d]:
            rs[half - 1, d, sub(i)] = part[half - 1, d, sub(i)].astype(bf16)
            back_copy(half - 1, d, i).start()
    for i in range(nx):
        far_copy(0 if i in early else 1, i).wait_recv()
    compute(0, (mz, lax.rem(mz + half, nz)))
    for i in range(nx):
        stage[sub(i)] = part[0, 1, sub(i)].astype(bf16)
        first_copy(0 if i in early else 1, i).start()

    def pass_on(s, d, i):
        rs[s, d, sub(i)] = (rs[s, d, sub(i)].astype(f32) + part[s, d, sub(i)]).astype(bf16)
        back_copy(s, d, i).start()

    for k in range(nx // 2):
        for d in range(2):
            i = (early, late)[d][k]
            first_copy(d, i).wait_recv()
            pass_on(half - 1, d, i)

    order = (list(late) + list(early), list(early) + list(late))

    @pl.loop(1, half - 1)
    def _(step):
        s = half - 1 - step
        for k in range(nx):
            for d in range(2):
                back_copy(s + 1, d, order[d][k]).wait_recv()
                pass_on(s, d, order[d][k])
        remote(ag.at[s], ag.at[s], ag_send.at[s + 1], ag_recv.at[s, 0, 0], right).wait_send()

    for i in range(1, nx):
        gate_copy(i).wait_recv()

    def y_copy(h, i):
        device = ((sec_up, sec_down)[h], columns[i] * nz + mz)
        return remote(ysend.at[h, sub(i)], yrecv.at[h, sub_at(mx)], y_send.at[h], y_recv.at[h, mx], device)

    for k in range(nx):
        i = (list(early) + list(late))[(k % 2) * (nx // 2) + k // 2]
        for d in range(2):
            back_copy(1, d, i).wait_recv()
        gate = gown[sub(i), 0:1]

        @pl.loop(0, fold // ftile)
        def _(step):
            halves = []
            for side in range(2):
                cols = pl.ds(pl.multiple_of(side * fold + step * ftile, 128), ftile)
                total = part[0, 0, sub(i), cols]
                for d in range(2):
                    total = total + rs[0, d, sub(i), cols].astype(f32)
                halves.append(ag[0, 0, sub(i), cols].astype(f32) + gate * total)
            cols = pl.ds(pl.multiple_of(step * ftile, 128), ftile)
            for h in range(2):
                picked = [value[h * CAP : (h + 1) * CAP] for value in halves]
                ysend[h, sub(i), cols] = jnp.concatenate(picked, axis=0).astype(bf16)

        for h in range(2):
            y_copy(h, i).start()

    for copy in near_copies:
        copy.wait()
    for h in range(2):
        for e in range(nx):
            remote(ysend.at[h, sub(e)], yrecv.at[h, sub(e)], y_send.at[h], y_recv.at[h, e], next_of[h]).wait_recv()
        place = near_plr[h]
        with_share = jnp.max(place.astype(f32), axis=1, keepdims=True) > 0.5
        for side in range(2):
            spots = place[:, side * span : (side + 1) * span]

            @pl.loop(0, fold // ftile)
            def _(step):
                part_cols = pl.ds(pl.multiple_of(step * ftile, 128), ftile)
                cols = pl.ds(pl.multiple_of(side * fold + step * ftile, 128), ftile)
                moved = jnp.dot(spots, yrecv[h, :, part_cols], preferred_element_type=f32)
                kept = near[h, :, cols].astype(f32)
                obuf[h, :, cols] = jnp.where(with_share, moved, kept).astype(bf16)

        pltpu.make_async_copy(obuf.at[h], (outf_hbm, outb_hbm)[h], out_sem.at[h]).start()

    for i in range(1, nx):
        row_copy(i).wait_send()
        gate_copy(i).wait_send()
    for d in range(2):
        remote(ag.at[0, 0], ag.at[1, d], ag_send.at[d], ag_recv.at[1, d, 0], right).wait_send()
        far_rows = pl.ds((early, late)[d][0] * SUB, SUB * (nx // 2))
        far = ag.at[half - 1, d, far_rows]
        remote(far, far, ag_send.at[half + d], ag_recv.at[0, 1, 0], right).wait_send()
        remote(ysend.at[d], yrecv.at[d], y_send.at[d], y_recv.at[d, 0], right).wait_send()
    remote(stage, rs.at[0, 0], rs_send.at[0], rs_recv.at[0, 0, 0], right).wait_send()
    for s in range(1, half):
        remote(rs.at[s], rs.at[s - 1], rs_send.at[s], rs_recv.at[0, 0, 0], right).wait_send()
    for h in range(2):
        pltpu.make_async_copy(obuf.at[h], (outf_hbm, outb_hbm)[h], out_sem.at[h]).wait()


def per_device(x_fwd, ids_fwd, gates_fwd, dy_bwd, ids_bwd, gates_bwd, saved_hidden, w_up, w_down):
    nsec = lax.axis_size("section")
    devices = lax.axis_size("expert")
    hid = w_up.shape[2]
    nz = FF // hid
    nx = devices // nz
    half = nz // 2
    tokens, width = x_fwd.shape[1:]
    span = SUB * nx
    any_space = pl.BlockSpec(memory_space=pl.ANY)
    vmem = pl.BlockSpec(memory_space=pltpu.VMEM)
    dma = pltpu.SemaphoreType.DMA
    outs = pl.pallas_call(
        functools.partial(kernel, nsec, nx, nz),
        out_shape=[jax.ShapeDtypeStruct((tokens, width), bf16)] * 2,
        in_specs=[any_space, any_space, vmem, vmem, vmem, vmem, any_space, any_space, any_space],
        out_specs=[any_space, any_space],
        scratch_shapes=[
            pltpu.VMEM((2, tokens, width), bf16),
            pltpu.VMEM((span, width), bf16),
            pltpu.VMEM((span, 128), f32),
            pltpu.VMEM((span, 128), f32),
            pltpu.VMEM((width, 2 * hid), bf16),
            pltpu.VMEM((2 * hid, width), bf16),
            pltpu.VMEM((nx, nz, CAP, hid), f32),
            pltpu.VMEM((half, 2, span, width), bf16),
            pltpu.VMEM((half, 2, span, width), bf16),
            pltpu.VMEM((span, width), bf16),
            pltpu.VMEM((half, 2, span, width), f32),
            pltpu.VMEM((2, tokens, 2 * span), bf16),
            pltpu.VMEM((2, tokens, width), bf16),
            pltpu.VMEM((2, tokens, 2 * span), bf16),
            pltpu.VMEM((2, span, width // 2), bf16),
            pltpu.VMEM((2, span, width // 2), bf16),
            pltpu.VMEM((2, tokens, width), bf16),
            dma((5,)), dma((2,)),
            dma((nx - 1,)), dma((nx - 1,)), dma((nx - 1,)), dma((nx - 1,)),
            dma((half + 2,)), dma((half, 2, nx)),
            dma((half,)), dma((half, 2, nx)),
            dma((2, 2)), dma((2, 2)), dma((2,)), dma((2, nx)),
        ],
        compiler_params=pltpu.CompilerParams(
            collective_id=0, has_side_effects=True, vmem_limit_bytes=56 * 1024 * 1024
        ),
    )(
        x_fwd[0], dy_bwd[0], ids_fwd[0], gates_fwd[0], ids_bwd[0], gates_bwd[0],
        saved_hidden[0].reshape(nx, nz, CAP, hid), w_up[0], w_down[0],
    )
    return (outs[0][None], outs[1][None])


def solution(mesh):
    in_specs = (
        P("section", "expert", None),
        P("section", "expert", None),
        P("section", "expert", None),
        P("section", "expert", None),
        P("section", "expert", None),
        P("section", "expert", None),
        P("section", None, "expert"),
        P("section", None, "expert"),
        P("section", "expert", None),
    )
    out_specs = (P("section", "expert", None), P("section", "expert", None))
    return jax.shard_map(
        per_device, mesh=mesh, in_specs=in_specs, out_specs=out_specs, check_vma=False
    )
```

```python
import functools

import jax
import jax.numpy as jnp
from jax import lax
from jax.experimental import pallas as pl
from jax.experimental.pallas import tpu as pltpu
from jax.sharding import PartitionSpec as P

MESH = pl.DeviceIdType.MESH
CAP = 8
SUB = 2 * CAP
FF = 2048
f32 = jnp.float32
bf16 = jnp.bfloat16


def tile_of(width):
    return 512 if width % 512 == 0 else 128


def routing(ids_f, gates_f, ids_b, gates_b, window):
    rows = ids_f.shape[1]
    routed, gates = [], []
    for ids, values in ((ids_f, gates_f), (ids_b, gates_b)):
        for e in range(window):
            match = ids == e
            routed.append(jnp.max(jnp.where(match, 1.0, 0.0), axis=0, keepdims=True))
            gates.append(jnp.sum(jnp.where(match, values, 0.0), axis=0, keepdims=True))
    earlier = lax.broadcasted_iota(jnp.int32, (rows, rows), 0) < lax.broadcasted_iota(
        jnp.int32, (rows, rows), 1
    )
    position = jnp.dot(
        jnp.concatenate(routed, axis=0).astype(bf16),
        jnp.where(earlier, 1.0, 0.0).astype(bf16),
        preferred_element_type=f32,
    )
    slot = lax.broadcasted_iota(jnp.int32, (CAP, rows), 0).astype(f32)
    places, weights = [], []
    for k in range(2 * window):
        place = jnp.where((position[k : k + 1] == slot) & (routed[k] > 0.5), 1.0, 0.0)
        places.append(place)
        weights.append(jnp.sum(place * gates[k], axis=1, keepdims=True))
    return (places[:window], places[window:]), (weights[:window], weights[window:])


def kernel(
    nsec, nx, nz,
    x_hbm, dy_hbm, idf_hbm, gf_hbm, idb_hbm, gb_hbm, saved_hbm, up_hbm, down_hbm,
    near, near_plr, yrecv,
    xin, ids, gates, rows, gall, gown, upw, downw, saved, ag, rs, stage, part, plr, ysend,
    load_sem, xs_send, xs_recv, gs_send, gs_recv, ag_send, ag_recv, rs_send, rs_recv,
    near_send, near_recv, y_send, y_recv,
):
    half = nz // 2
    width = xin.shape[2]
    span = SUB * nx
    fold = width // 2
    hid = upw.shape[1] // 2
    tile = tile_of(width)
    seq = (0, 1, 3, 2) if nx == 4 else tuple(range(nx))
    early = range(nx // 2)
    late = range(nx // 2, nx)

    sec = lax.axis_index("section")
    me = lax.axis_index("expert")
    mx, mz = lax.div(me, nz), lax.rem(me, nz)
    right = (sec, mx * nz + lax.rem(mz + 1, nz))
    left = (sec, mx * nz + lax.rem(mz + nz - 1, nz))
    sec_up, sec_down = lax.rem(sec + 1, nsec), lax.rem(sec + nsec - 1, nsec)
    columns = [lax.rem(mx + i, nx) for i in range(nx)]
    targets = [lax.rem(mx + nx - i, nx) for i in range(nx)]
    out_way = (right, left)
    back_way = (left, right)

    def remote(src, dst, send, recv, device):
        return pltpu.make_async_remote_copy(
            src_ref=src, dst_ref=dst, send_sem=send, recv_sem=recv, device_id=device, device_id_type=MESH
        )

    def sub(i):
        return pl.ds(i * SUB, SUB)

    def sub_at(index):
        return pl.ds(pl.multiple_of(index * SUB, SUB), SUB)

    loads = [
        pltpu.make_async_copy(src, dst, load_sem.at[k])
        for k, (src, dst) in enumerate((
            (idf_hbm, ids.at[0]), (gf_hbm, gates.at[0]), (idb_hbm, ids.at[1]), (gb_hbm, gates.at[1]),
            (x_hbm, xin.at[0]), (dy_hbm, xin.at[1]),
            (up_hbm, upw.at[:, pl.ds(0, hid)]), (down_hbm, downw.at[pl.ds(0, hid)]), (saved_hbm, saved),
        ))
    ]
    for load in loads:
        load.start()

    peers = [right, left]
    peers += [(sec, columns[i] * nz + mz) for i in range(1, nx)]
    peers += [(s, columns[i] * nz + mz) for s in (sec_up, sec_down) for i in range(nx)]
    barrier = pltpu.get_barrier_semaphore()
    for peer in peers:
        pl.semaphore_signal(barrier, inc=1, device_id=peer, device_id_type=MESH)

    for load in loads[:4]:
        load.wait()
    places, weights = routing(ids[0], gates[0], ids[1], gates[1], nx)
    blank = jnp.zeros_like(places[0][0])
    chosen_f = jnp.concatenate([piece for e in range(nx) for piece in (places[0][e], blank)]).astype(bf16)
    chosen_b = jnp.concatenate([piece for e in range(nx) for piece in (blank, places[1][e])]).astype(bf16)
    weight = jnp.concatenate([weights[h][e] for e in range(nx) for h in range(2)])
    gall[...] = jnp.broadcast_to(weight, gall.shape)
    for load in loads[4:6]:
        load.wait()

    @pl.loop(0, width // tile)
    def _(step):
        cols = pl.ds(pl.multiple_of(step * tile, tile), tile)
        rows[:, cols] = (
            jnp.dot(chosen_f, xin[0, :, cols], preferred_element_type=f32)
            + jnp.dot(chosen_b, xin[1, :, cols], preferred_element_type=f32)
        ).astype(bf16)

    ag[0, 0, sub(0)] = rows[sub_at(mx)]
    gown[sub(0)] = gall[sub_at(mx)]
    pl.semaphore_wait(barrier, len(peers))

    def row_copy(i):
        device = (sec, targets[i] * nz + mz)
        return remote(
            rows.at[sub_at(targets[i])], ag.at[0, 0, sub(i)], xs_send.at[i - 1], xs_recv.at[i - 1], device
        )

    def gate_copy(i):
        device = (sec, targets[i] * nz + mz)
        return remote(
            gall.at[sub_at(targets[i])], gown.at[sub(i)], gs_send.at[i - 1], gs_recv.at[i - 1], device
        )

    def out_copy(s, d, i, own=False):
        src = ag.at[0, 0, sub(i)] if own else ag.at[s, d, sub(i)]
        send = ag_send.at[d] if own else ag_send.at[s + 1]
        return remote(src, ag.at[s + 1, d, sub(i)], send, ag_recv.at[s + 1, d, i], out_way[d])

    def far_copy(d, i):
        send = ag_send.at[half if d == 0 else half + 1]
        return remote(ag.at[half - 1, d, sub(i)], ag.at[0, 1, sub(i)], send, ag_recv.at[0, 1, i], out_way[d])

    for d in range(2):
        out_copy(0, d, 0, own=True).start()
    for i in seq[1:]:
        row_copy(i).start()
    for i in range(1, nx):
        gate_copy(i).start()

    next_of = ((sec_up, me), (sec_down, me))
    near_copies = [
        remote(src.at[h], dst.at[h], near_send.at[h, k], near_recv.at[h, k], next_of[h])
        for h in range(2)
        for k, (src, dst) in enumerate(((xin, near), (plr, near_plr)))
    ]
    near_copies[0].start()
    near_copies[2].start()

    for i in seq[1:]:
        row_copy(i).wait_recv()
        for d in range(2):
            out_copy(0, d, i, own=True).start()

    for load in loads[6:]:
        load.wait()

    @pl.loop(0, width // tile)
    def _(step):
        cols = pl.ds(pl.multiple_of(step * tile, tile), tile)
        upw[cols, pl.ds(hid, hid)] = downw[pl.ds(0, hid), cols].T
        downw[pl.ds(hid, hid), cols] = upw[cols, pl.ds(0, hid)].T

    @pl.loop(0, nx)
    def _(column):
        value = saved[column]
        sig = jax.nn.sigmoid(value)
        saved[column] = sig * (1.0 + value * (1.0 - sig))

    for h in range(2):
        sides = [[places[h][e], blank] for e in range(nx)], [[blank, places[h][e]] for e in range(nx)]
        spots = jnp.concatenate([piece for side in sides for pair in side for piece in pair])
        plr[h] = spots.T.astype(bf16)
        near_copies[2 * h + 1].start()

    def compute(s, sources):
        def add_up(step, total):
            cols = pl.ds(pl.multiple_of(step * tile, tile), tile)
            block = ag[s, :, :, cols].reshape(2 * span, tile)
            return total + jnp.dot(block, upw[cols, :], preferred_element_type=f32)

        total = lax.fori_loop(0, width // tile, add_up, jnp.zeros((2 * span, 2 * hid), f32))
        total = total.reshape(2 * nx, 2, CAP, 2 * hid)
        forward = total[:, 0, :, :hid]
        forward = forward * jax.nn.sigmoid(forward)
        slope = jnp.stack([saved[columns[i], source] for source in sources for i in range(nx)])
        backward = total[:, 1, :, hid:] * slope
        none = jnp.zeros_like(forward)
        inner = jnp.stack(
            [jnp.concatenate([forward, none], axis=-1), jnp.concatenate([none, backward], axis=-1)], axis=1
        )
        inner = inner.reshape(2 * span, 2 * hid).astype(bf16)

        @pl.loop(0, width // tile)
        def _(step):
            cols = pl.ds(pl.multiple_of(step * tile, tile), tile)
            result = jnp.dot(inner, downw[:, cols], preferred_element_type=f32)
            part[s, :, :, cols] = result.reshape(2, span, tile)

    def both(s):
        return (lax.rem(mz + nz - s, nz), lax.rem(mz + s, nz))

    @pl.loop(1, half - 1)
    def _(s):
        for i in seq:
            for d in range(2):
                out_copy(s - 1, d, i).wait_recv()
                out_copy(s, d, i).start()
        compute(s, both(s))

    for i in seq:
        for d in range(2):
            out_copy(half - 2, d, i).wait_recv()
            if i in (early, late)[d]:
                far_copy(d, i).start()
    compute(half - 1, both(half - 1))

    def back_copy(s, d, i):
        return remote(
            rs.at[s, d, sub(i)], rs.at[s - 1, d, sub(i)], rs_send.at[s], rs_recv.at[s - 1, d, i], back_way[d]
        )

    def first_copy(d, i):
        return remote(stage.at[sub(i)], rs.at[half - 1, d, sub(i)], rs_send.at[0], rs_recv.at[half - 1, d, i], back_way[d])

    for d in range(2):
        for i in (late, early)[d]:
            rs[half - 1, d, sub(i)] = part[half - 1, d, sub(i)].astype(bf16)
            back_copy(half - 1, d, i).start()
    for i in range(nx):
        far_copy(0 if i in early else 1, i).wait_recv()
    compute(0, (mz, lax.rem(mz + half, nz)))
    for i in range(nx):
        stage[sub(i)] = part[0, 1, sub(i)].astype(bf16)
        first_copy(0 if i in early else 1, i).start()

    def pass_on(s, d, i):
        rs[s, d, sub(i)] = (rs[s, d, sub(i)].astype(f32) + part[s, d, sub(i)]).astype(bf16)
        back_copy(s, d, i).start()

    for k in range(nx // 2):
        for d in range(2):
            i = (early, late)[d][k]
            first_copy(d, i).wait_recv()
            pass_on(half - 1, d, i)

    order = (list(late) + list(early), list(early) + list(late))

    @pl.loop(1, half - 1)
    def _(step):
        s = half - 1 - step
        for k in range(nx):
            for d in range(2):
                back_copy(s + 1, d, order[d][k]).wait_recv()
                pass_on(s, d, order[d][k])
        remote(ag.at[s], ag.at[s], ag_send.at[s + 1], ag_recv.at[s, 0, 0], right).wait_send()

    for i in range(1, nx):
        gate_copy(i).wait_recv()

    def y_copy(h, i):
        device = ((sec_up, sec_down)[h], columns[i] * nz + mz)
        return remote(ysend.at[h, sub(i)], yrecv.at[h, sub_at(mx)], y_send.at[h], y_recv.at[h, mx], device)

    for k in range(nx):
        i = (list(early) + list(late))[(k % 2) * (nx // 2) + k // 2]
        for d in range(2):
            back_copy(1, d, i).wait_recv()
        gate = gown[sub(i), 0:1]

        total = part[0, 0, sub(i)]
        for d in range(2):
            total = total + rs[0, d, sub(i)].astype(f32)
        value = ag[0, 0, sub(i)].astype(f32) + gate * total
        for h in range(2):
            picked = value[h * CAP : (h + 1) * CAP]
            ysend[h, sub(i)] = jnp.concatenate([picked[:, :fold], picked[:, fold:]], axis=0).astype(bf16)

        for h in range(2):
            y_copy(h, i).start()

    for copy in near_copies:
        copy.wait()
    for h in range(2):
        for e in range(nx):
            remote(ysend.at[h, sub(e)], yrecv.at[h, sub(e)], y_send.at[h], y_recv.at[h, e], next_of[h]).wait_recv()

    for i in range(1, nx):
        row_copy(i).wait_send()
        gate_copy(i).wait_send()
    for d in range(2):
        remote(ag.at[0, 0], ag.at[1, d], ag_send.at[d], ag_recv.at[1, d, 0], right).wait_send()
        far_rows = pl.ds((early, late)[d][0] * SUB, SUB * (nx // 2))
        far = ag.at[half - 1, d, far_rows]
        remote(far, far, ag_send.at[half + d], ag_recv.at[0, 1, 0], right).wait_send()
        remote(ysend.at[d], yrecv.at[d], y_send.at[d], y_recv.at[d, 0], right).wait_send()
    remote(stage, rs.at[0, 0], rs_send.at[0], rs_recv.at[0, 0, 0], right).wait_send()
    for s in range(1, half):
        remote(rs.at[s], rs.at[s - 1], rs_send.at[s], rs_recv.at[0, 0, 0], right).wait_send()

def place_rows(near, near_plr, yrecv, outf, outb, rows, places, moved, done, load_sem, out_sem):
    width = rows.shape[2]
    fold = width // 2
    span = moved.shape[1]
    first = [
        pltpu.make_async_copy(near_plr, places, load_sem.at[0]),
        pltpu.make_async_copy(yrecv, moved, load_sem.at[1]),
    ]
    sides = [(h, side, pl.ds(side * fold, fold)) for h in range(2) for side in range(2)]
    loads = [
        pltpu.make_async_copy(near.at[h, :, cols], rows.at[h, :, cols], load_sem.at[2 + 2 * h + side])
        for h, side, cols in sides
    ]
    stores = [
        pltpu.make_async_copy(done.at[h, :, cols], (outf, outb)[h].at[:, cols], out_sem.at[2 * h + side])
        for h, side, cols in sides
    ]
    for load in first + loads:
        load.start()
    for load in first:
        load.wait()
    for (h, side, cols), load, store in zip(sides, loads, stores):
        place = places[h]
        with_share = jnp.max(place.astype(f32), axis=1, keepdims=True) > 0.5
        spots = place[:, side * span : (side + 1) * span]
        share = jnp.dot(spots, moved[h], preferred_element_type=f32)
        load.wait()
        done[h, :, cols] = jnp.where(with_share, share, rows[h, :, cols].astype(f32)).astype(bf16)
        store.start()
    for store in stores:
        store.wait()


def per_device(x_fwd, ids_fwd, gates_fwd, dy_bwd, ids_bwd, gates_bwd, saved_hidden, w_up, w_down):
    nsec = lax.axis_size("section")
    devices = lax.axis_size("expert")
    hid = w_up.shape[2]
    nz = FF // hid
    nx = devices // nz
    half = nz // 2
    tokens, width = x_fwd.shape[1:]
    span = SUB * nx
    choices = ids_fwd.shape[2]
    any_space = pl.BlockSpec(memory_space=pl.ANY)
    dma = pltpu.SemaphoreType.DMA
    near, near_plr, yrecv = pl.pallas_call(
        functools.partial(kernel, nsec, nx, nz),
        out_shape=[
            jax.ShapeDtypeStruct((2, tokens, width), bf16),
            jax.ShapeDtypeStruct((2, tokens, 2 * span), bf16),
            jax.ShapeDtypeStruct((2, span, width // 2), bf16),
        ],
        in_specs=[any_space] * 9,
        out_specs=[any_space] * 3,
        scratch_shapes=[
            pltpu.VMEM((2, tokens, width), bf16),
            pltpu.VMEM((2, choices, tokens), jnp.int32),
            pltpu.VMEM((2, choices, tokens), f32),
            pltpu.VMEM((span, width), bf16),
            pltpu.VMEM((span, 128), f32),
            pltpu.VMEM((span, 128), f32),
            pltpu.VMEM((width, 2 * hid), bf16),
            pltpu.VMEM((2 * hid, width), bf16),
            pltpu.VMEM((nx, nz, CAP, hid), f32),
            pltpu.VMEM((half, 2, span, width), bf16),
            pltpu.VMEM((half, 2, span, width), bf16),
            pltpu.VMEM((span, width), bf16),
            pltpu.VMEM((half, 2, span, width), f32),
            pltpu.VMEM((2, tokens, 2 * span), bf16),
            pltpu.VMEM((2, span, width // 2), bf16),
            dma((9,)),
            dma((nx - 1,)), dma((nx - 1,)), dma((nx - 1,)), dma((nx - 1,)),
            dma((half + 2,)), dma((half, 2, nx)),
            dma((half,)), dma((half, 2, nx)),
            dma((2, 2)), dma((2, 2)), dma((2,)), dma((2, nx)),
        ],
        compiler_params=pltpu.CompilerParams(
            collective_id=0, has_side_effects=True, vmem_limit_bytes=56 * 1024 * 1024
        ),
    )(
        x_fwd[0], dy_bwd[0], ids_fwd[0].T, gates_fwd[0].T, ids_bwd[0].T, gates_bwd[0].T,
        saved_hidden[0].reshape(nx, nz, CAP, hid), w_up[0], w_down[0],
    )
    outs = pl.pallas_call(
        place_rows,
        out_shape=[jax.ShapeDtypeStruct((tokens, width), bf16)] * 2,
        in_specs=[any_space] * 3,
        out_specs=[any_space] * 2,
        scratch_shapes=[
            pltpu.VMEM((2, tokens, width), bf16),
            pltpu.VMEM((2, tokens, 2 * span), bf16),
            pltpu.VMEM((2, span, width // 2), bf16),
            pltpu.VMEM((2, tokens, width), bf16),
            dma((6,)), dma((4,)),
        ],
        compiler_params=pltpu.CompilerParams(vmem_limit_bytes=60 * 1024 * 1024),
    )(near, near_plr, yrecv)
    return (outs[0][None], outs[1][None])


def solution(mesh):
    in_specs = (
        P("section", "expert", None),
        P("section", "expert", None),
        P("section", "expert", None),
        P("section", "expert", None),
        P("section", "expert", None),
        P("section", "expert", None),
        P("section", None, "expert"),
        P("section", None, "expert"),
        P("section", "expert", None),
    )
    out_specs = (P("section", "expert", None), P("section", "expert", None))
    return jax.shard_map(
        per_device, mesh=mesh, in_specs=in_specs, out_specs=out_specs, check_vma=False
    )
```

```python
import functools

import jax
import jax.numpy as jnp
from jax import lax
from jax.experimental import pallas as pl
from jax.experimental.pallas import tpu as pltpu
from jax.sharding import PartitionSpec as P

MESH = pl.DeviceIdType.MESH
CAP = 8
SUB = 2 * CAP
FF = 2048
f32 = jnp.float32
bf16 = jnp.bfloat16


def tile_of(width):
    return 512 if width % 512 == 0 else 128


def routing(ids_f, gates_f, ids_b, gates_b, window):
    rows = ids_f.shape[1]
    routed, gates = [], []
    for ids, values in ((ids_f, gates_f), (ids_b, gates_b)):
        for e in range(window):
            match = ids == e
            routed.append(jnp.max(jnp.where(match, 1.0, 0.0), axis=0, keepdims=True))
            gates.append(jnp.sum(jnp.where(match, values, 0.0), axis=0, keepdims=True))
    earlier = lax.broadcasted_iota(jnp.int32, (rows, rows), 0) < lax.broadcasted_iota(
        jnp.int32, (rows, rows), 1
    )
    position = jnp.dot(
        jnp.concatenate(routed, axis=0).astype(bf16),
        jnp.where(earlier, 1.0, 0.0).astype(bf16),
        preferred_element_type=f32,
    )
    slot = lax.broadcasted_iota(jnp.int32, (CAP, rows), 0).astype(f32)
    places, weights = [], []
    for k in range(2 * window):
        place = jnp.where((position[k : k + 1] == slot) & (routed[k] > 0.5), 1.0, 0.0)
        places.append(place)
        weights.append(jnp.sum(place * gates[k], axis=1, keepdims=True))
    return (places[:window], places[window:]), (weights[:window], weights[window:])


def kernel(
    nsec, nx, nz,
    x_hbm, dy_hbm, idf_hbm, gf_hbm, idb_hbm, gb_hbm, saved_hbm, up_hbm, down_hbm,
    near, near_plr, yrecv,
    xin, ids, gates, rows, gall, gown, upw, downw, saved, ag, rs, stage, part, plr, ysend,
    load_sem, xs_send, xs_recv, gs_send, gs_recv, ag_send, ag_recv, rs_send, rs_recv,
    near_send, near_recv, y_send, y_recv,
):
    half = nz // 2
    width = xin.shape[2]
    span = SUB * nx
    fold = width // 2
    hid = upw.shape[1] // 2
    tile = tile_of(width)
    seq = (0, 1, 3, 2) if nx == 4 else tuple(range(nx))
    back_seq = seq[::-1]
    sides = (pl.ds(0, fold), pl.ds(fold, fold))

    sec = lax.axis_index("section")
    me = lax.axis_index("expert")
    mx, mz = lax.div(me, nz), lax.rem(me, nz)
    right = (sec, mx * nz + lax.rem(mz + 1, nz))
    left = (sec, mx * nz + lax.rem(mz + nz - 1, nz))
    sec_up, sec_down = lax.rem(sec + 1, nsec), lax.rem(sec + nsec - 1, nsec)
    columns = [lax.rem(mx + i, nx) for i in range(nx)]
    targets = [lax.rem(mx + nx - i, nx) for i in range(nx)]
    out_way = (right, left)
    back_way = (left, right)

    def remote(src, dst, send, recv, device):
        return pltpu.make_async_remote_copy(
            src_ref=src, dst_ref=dst, send_sem=send, recv_sem=recv, device_id=device, device_id_type=MESH
        )

    def sub(i):
        return pl.ds(i * SUB, SUB)

    def sub_at(index):
        return pl.ds(pl.multiple_of(index * SUB, SUB), SUB)

    loads = [
        pltpu.make_async_copy(src, dst, load_sem.at[k])
        for k, (src, dst) in enumerate((
            (idf_hbm, ids.at[0]), (gf_hbm, gates.at[0]), (idb_hbm, ids.at[1]), (gb_hbm, gates.at[1]),
            (x_hbm, xin.at[0]), (dy_hbm, xin.at[1]),
            (up_hbm, upw.at[:, pl.ds(0, hid)]), (down_hbm, downw.at[pl.ds(0, hid)]), (saved_hbm, saved),
        ))
    ]
    for load in loads:
        load.start()

    peers = [right, left]
    peers += [(sec, columns[i] * nz + mz) for i in range(1, nx)]
    peers += [(s, columns[i] * nz + mz) for s in (sec_up, sec_down) for i in range(nx)]
    barrier = pltpu.get_barrier_semaphore()
    for peer in peers:
        pl.semaphore_signal(barrier, inc=1, device_id=peer, device_id_type=MESH)

    for load in loads[:4]:
        load.wait()
    places, weights = routing(ids[0], gates[0], ids[1], gates[1], nx)
    blank = jnp.zeros_like(places[0][0])
    chosen_f = jnp.concatenate([piece for e in range(nx) for piece in (places[0][e], blank)]).astype(bf16)
    chosen_b = jnp.concatenate([piece for e in range(nx) for piece in (blank, places[1][e])]).astype(bf16)
    weight = jnp.concatenate([weights[h][e] for e in range(nx) for h in range(2)])
    gall[...] = jnp.broadcast_to(weight, gall.shape)
    for load in loads[4:6]:
        load.wait()

    @pl.loop(0, width // tile)
    def _(step):
        cols = pl.ds(pl.multiple_of(step * tile, tile), tile)
        rows[:, cols] = (
            jnp.dot(chosen_f, xin[0, :, cols], preferred_element_type=f32)
            + jnp.dot(chosen_b, xin[1, :, cols], preferred_element_type=f32)
        ).astype(bf16)

    ag[0, 0, sub(0)] = rows[sub_at(mx)]
    gown[sub(0)] = gall[sub_at(mx)]
    pl.semaphore_wait(barrier, len(peers))

    def row_copy(i):
        device = (sec, targets[i] * nz + mz)
        return remote(
            rows.at[sub_at(targets[i])], ag.at[0, 0, sub(i)], xs_send.at[i - 1], xs_recv.at[i - 1], device
        )

    def gate_copy(i):
        device = (sec, targets[i] * nz + mz)
        return remote(
            gall.at[sub_at(targets[i])], gown.at[sub(i)], gs_send.at[i - 1], gs_recv.at[i - 1], device
        )

    def out_copy(s, d, i, own=False):
        src = ag.at[0, 0, sub(i)] if own else ag.at[s, d, sub(i)]
        send = ag_send.at[d] if own else ag_send.at[s + 1]
        return remote(src, ag.at[s + 1, d, sub(i)], send, ag_recv.at[s + 1, d, i], out_way[d])

    def far_copy(d, i):
        src, dst = ag.at[half - 1, d, sub(i), sides[d]], ag.at[0, 1, sub(i), sides[d]]
        return remote(src, dst, ag_send.at[half + d], ag_recv.at[0, d, i], out_way[d])

    for d in range(2):
        out_copy(0, d, 0, own=True).start()
    for i in seq[1:]:
        row_copy(i).start()
    for i in range(1, nx):
        gate_copy(i).start()

    next_of = ((sec_up, me), (sec_down, me))
    near_copies = [
        remote(src.at[h], dst.at[h], near_send.at[h, k], near_recv.at[h, k], next_of[h])
        for h in range(2)
        for k, (src, dst) in enumerate(((xin, near), (plr, near_plr)))
    ]
    near_copies[0].start()
    near_copies[2].start()

    for i in seq[1:]:
        row_copy(i).wait_recv()
        for d in range(2):
            out_copy(0, d, i, own=True).start()

    for load in loads[6:]:
        load.wait()

    @pl.loop(0, width // tile)
    def _(step):
        cols = pl.ds(pl.multiple_of(step * tile, tile), tile)
        upw[cols, pl.ds(hid, hid)] = downw[pl.ds(0, hid), cols].T
        downw[pl.ds(hid, hid), cols] = upw[cols, pl.ds(0, hid)].T

    @pl.loop(0, nx)
    def _(column):
        value = saved[column]
        sig = jax.nn.sigmoid(value)
        saved[column] = sig * (1.0 + value * (1.0 - sig))

    for h in range(2):
        pairs = [[places[h][e], blank] for e in range(nx)] + [[blank, places[h][e]] for e in range(nx)]
        spots = jnp.concatenate([piece for pair in pairs for piece in pair])
        plr[h] = spots.T.astype(bf16)
        near_copies[2 * h + 1].start()

    def compute(s, first, sources):
        count = len(sources)
        blocks = pl.ds(first, count)

        def add_up(step, total):
            cols = pl.ds(pl.multiple_of(step * tile, tile), tile)
            block = ag[s, blocks, :, cols].reshape(count * span, tile)
            return total + jnp.dot(block, upw[cols, :], preferred_element_type=f32)

        total = lax.fori_loop(0, width // tile, add_up, jnp.zeros((count * span, 2 * hid), f32))
        total = total.reshape(count * nx, 2, CAP, 2 * hid)
        forward = total[:, 0, :, :hid]
        forward = forward * jax.nn.sigmoid(forward)
        slope = jnp.stack([saved[columns[i], source] for source in sources for i in range(nx)])
        backward = total[:, 1, :, hid:] * slope
        none = jnp.zeros_like(forward)
        inner = jnp.stack(
            [jnp.concatenate([forward, none], axis=-1), jnp.concatenate([none, backward], axis=-1)], axis=1
        )
        inner = inner.reshape(count * span, 2 * hid).astype(bf16)

        @pl.loop(0, width // tile)
        def _(step):
            cols = pl.ds(pl.multiple_of(step * tile, tile), tile)
            result = jnp.dot(inner, downw[:, cols], preferred_element_type=f32)
            part[s, blocks, :, cols] = result.reshape(count, span, tile)

    def both(s):
        return (lax.rem(mz + nz - s, nz), lax.rem(mz + s, nz))

    @pl.loop(1, half - 1)
    def _(s):
        for i in seq:
            for d in range(2):
                out_copy(s - 1, d, i).wait_recv()
                out_copy(s, d, i).start()
        compute(s, 0, both(s))

    for i in seq:
        for d in range(2):
            out_copy(half - 2, d, i).wait_recv()
            far_copy(d, i).start()
    compute(half - 1, 0, both(half - 1))

    def back_copy(s, d, i):
        return remote(
            rs.at[s, d, sub(i)], rs.at[s - 1, d, sub(i)], rs_send.at[s], rs_recv.at[s - 1, d, i], back_way[d]
        )

    def half_copy(d, i, side):
        src, dst = rs.at[half - 1, d, sub(i), sides[side]], rs.at[half - 2, d, sub(i), sides[side]]
        return remote(src, dst, rs_send.at[half - 1], rs_recv.at[half - 2, d, i], back_way[d])

    def first_copy(d, i):
        src, dst = stage.at[sub(i), sides[d]], rs.at[half - 1, d, sub(i), sides[d]]
        return remote(src, dst, rs_send.at[0], rs_recv.at[half - 1, d, i], back_way[d])

    for i in back_seq:
        for d in range(2):
            cols = sides[1 - d]
            rs[half - 1, d, sub(i), cols] = part[half - 1, d, sub(i), cols].astype(bf16)
            half_copy(d, i, 1 - d).start()
    for i in seq:
        for d in range(2):
            far_copy(d, i).wait_recv()
    compute(0, 1, (lax.rem(mz + half, nz),))
    for i in back_seq:
        stage[sub(i)] = part[0, 1, sub(i)].astype(bf16)
        for d in range(2):
            first_copy(d, i).start()
    compute(0, 0, (mz,))
    for i in back_seq:
        for d in range(2):
            cols = sides[d]
            first_copy(d, i).wait_recv()
            here = rs[half - 1, d, sub(i), cols].astype(f32) + part[half - 1, d, sub(i), cols]
            rs[half - 1, d, sub(i), cols] = here.astype(bf16)
            half_copy(d, i, d).start()

    @pl.loop(1, half - 1)
    def _(step):
        s = half - 1 - step
        for i in back_seq:
            for d in range(2):
                back_copy(s + 1, d, i).wait_recv()
                rs[s, d, sub(i)] = (rs[s, d, sub(i)].astype(f32) + part[s, d, sub(i)]).astype(bf16)
                back_copy(s, d, i).start()
        remote(ag.at[s], ag.at[s], ag_send.at[s + 1], ag_recv.at[s, 0, 0], right).wait_send()

    for i in range(1, nx):
        gate_copy(i).wait_recv()

    def y_copy(h, i):
        device = ((sec_up, sec_down)[h], columns[i] * nz + mz)
        return remote(ysend.at[h, sub(i)], yrecv.at[h, sub_at(mx)], y_send.at[h], y_recv.at[h, mx], device)

    for i in back_seq:
        for d in range(2):
            back_copy(1, d, i).wait_recv()
        gate = gown[sub(i), 0:1]

        total = part[0, 0, sub(i)]
        for d in range(2):
            total = total + rs[0, d, sub(i)].astype(f32)
        value = ag[0, 0, sub(i)].astype(f32) + gate * total
        for h in range(2):
            picked = value[h * CAP : (h + 1) * CAP]
            ysend[h, sub(i)] = jnp.concatenate([picked[:, :fold], picked[:, fold:]], axis=0).astype(bf16)

        for h in range(2):
            y_copy(h, i).start()

    for copy in near_copies:
        copy.wait()
    for h in range(2):
        for e in range(nx):
            remote(ysend.at[h, sub(e)], yrecv.at[h, sub(e)], y_send.at[h], y_recv.at[h, e], next_of[h]).wait_recv()

    for i in range(1, nx):
        row_copy(i).wait_send()
        gate_copy(i).wait_send()
    for d in range(2):
        remote(ag.at[0, 0], ag.at[1, d], ag_send.at[d], ag_recv.at[1, d, 0], right).wait_send()
        far = ag.at[half - 1, d, :, sides[d]]
        remote(far, far, ag_send.at[half + d], ag_recv.at[0, 1, 0], right).wait_send()
        remote(ysend.at[d], yrecv.at[d], y_send.at[d], y_recv.at[d, 0], right).wait_send()
    remote(stage, rs.at[0, 0], rs_send.at[0], rs_recv.at[0, 0, 0], right).wait_send()
    for s in range(1, half):
        remote(rs.at[s], rs.at[s - 1], rs_send.at[s], rs_recv.at[0, 0, 0], right).wait_send()

def place_rows(near, places, moved, outf, outb, done, out_sem):
    width = near.shape[2]
    fold = width // 2
    span = moved.shape[1]
    stores = []
    for h in range(2):
        place = places[h]
        with_share = jnp.max(place.astype(f32), axis=1, keepdims=True) > 0.5
        for side in range(2):
            cols = pl.ds(side * fold, fold)
            spots = place[:, side * span : (side + 1) * span]
            share = jnp.dot(spots, moved[h], preferred_element_type=f32)
            done[h, :, cols] = jnp.where(with_share, share, near[h, :, cols].astype(f32)).astype(bf16)
            store = pltpu.make_async_copy(done.at[h, :, cols], (outf, outb)[h].at[:, cols], out_sem.at[h, side])
            store.start()
            stores.append(store)
    for store in stores:
        store.wait()


def per_device(x_fwd, ids_fwd, gates_fwd, dy_bwd, ids_bwd, gates_bwd, saved_hidden, w_up, w_down):
    nsec = lax.axis_size("section")
    devices = lax.axis_size("expert")
    hid = w_up.shape[2]
    nz = FF // hid
    nx = devices // nz
    half = nz // 2
    tokens, width = x_fwd.shape[1:]
    span = SUB * nx
    choices = ids_fwd.shape[2]
    any_space = pl.BlockSpec(memory_space=pl.ANY)
    vmem = pl.BlockSpec(memory_space=pltpu.VMEM)
    dma = pltpu.SemaphoreType.DMA
    near, near_plr, yrecv = pl.pallas_call(
        functools.partial(kernel, nsec, nx, nz),
        out_shape=[
            pltpu.VMEM((2, tokens, width), bf16),
            pltpu.VMEM((2, tokens, 2 * span), bf16),
            pltpu.VMEM((2, span, width // 2), bf16),
        ],
        in_specs=[any_space] * 9,
        out_specs=[vmem] * 3,
        scratch_shapes=[
            pltpu.VMEM((2, tokens, width), bf16),
            pltpu.VMEM((2, choices, tokens), jnp.int32),
            pltpu.VMEM((2, choices, tokens), f32),
            pltpu.VMEM((span, width), bf16),
            pltpu.VMEM((span, 128), f32),
            pltpu.VMEM((span, 128), f32),
            pltpu.VMEM((width, 2 * hid), bf16),
            pltpu.VMEM((2 * hid, width), bf16),
            pltpu.VMEM((nx, nz, CAP, hid), f32),
            pltpu.VMEM((half, 2, span, width), bf16),
            pltpu.VMEM((half, 2, span, width), bf16),
            pltpu.VMEM((span, width), bf16),
            pltpu.VMEM((half, 2, span, width), f32),
            pltpu.VMEM((2, tokens, 2 * span), bf16),
            pltpu.VMEM((2, span, width // 2), bf16),
            dma((9,)),
            dma((nx - 1,)), dma((nx - 1,)), dma((nx - 1,)), dma((nx - 1,)),
            dma((half + 2,)), dma((half, 2, nx)),
            dma((half,)), dma((half, 2, nx)),
            dma((2, 2)), dma((2, 2)), dma((2,)), dma((2, nx)),
        ],
        compiler_params=pltpu.CompilerParams(
            collective_id=0, has_side_effects=True, vmem_limit_bytes=56 * 1024 * 1024
        ),
    )(
        x_fwd[0], dy_bwd[0], ids_fwd[0].T, gates_fwd[0].T, ids_bwd[0].T, gates_bwd[0].T,
        saved_hidden[0].reshape(nx, nz, CAP, hid), w_up[0], w_down[0],
    )
    outs = pl.pallas_call(
        place_rows,
        out_shape=[jax.ShapeDtypeStruct((tokens, width), bf16)] * 2,
        in_specs=[vmem] * 3,
        out_specs=[any_space] * 2,
        scratch_shapes=[pltpu.VMEM((2, tokens, width), bf16), dma((2, 2))],
        compiler_params=pltpu.CompilerParams(vmem_limit_bytes=32 * 1024 * 1024),
    )(*(pltpu.with_memory_space_constraint(v, pltpu.VMEM) for v in (near, near_plr, yrecv)))
    return (outs[0][None], outs[1][None])


def solution(mesh):
    in_specs = (
        P("section", "expert", None),
        P("section", "expert", None),
        P("section", "expert", None),
        P("section", "expert", None),
        P("section", "expert", None),
        P("section", "expert", None),
        P("section", None, "expert"),
        P("section", None, "expert"),
        P("section", "expert", None),
    )
    out_specs = (P("section", "expert", None), P("section", "expert", None))
    return jax.shard_map(
        per_device, mesh=mesh, in_specs=in_specs, out_specs=out_specs, check_vma=False
    )
```

```python
import functools

import jax
import jax.numpy as jnp
from jax import lax
from jax.experimental import pallas as pl
from jax.experimental.pallas import tpu as pltpu
from jax.sharding import PartitionSpec as P

MESH = pl.DeviceIdType.MESH
CAP = 8
SUB = 2 * CAP
FF = 2048
f32 = jnp.float32
bf16 = jnp.bfloat16


def tile_of(width):
    return 512 if width % 512 == 0 else 128


def routing(ids_f, gates_f, ids_b, gates_b, window):
    rows = ids_f.shape[1]
    routed, gates = [], []
    for ids, values in ((ids_f, gates_f), (ids_b, gates_b)):
        for e in range(window):
            match = ids == e
            routed.append(jnp.max(jnp.where(match, 1.0, 0.0), axis=0, keepdims=True))
            gates.append(jnp.sum(jnp.where(match, values, 0.0), axis=0, keepdims=True))
    earlier = lax.broadcasted_iota(jnp.int32, (rows, rows), 0) < lax.broadcasted_iota(
        jnp.int32, (rows, rows), 1
    )
    position = jnp.dot(
        jnp.concatenate(routed, axis=0).astype(bf16),
        jnp.where(earlier, 1.0, 0.0).astype(bf16),
        preferred_element_type=f32,
    )
    slot = lax.broadcasted_iota(jnp.int32, (CAP, rows), 0).astype(f32)
    places, weights = [], []
    for k in range(2 * window):
        place = jnp.where((position[k : k + 1] == slot) & (routed[k] > 0.5), 1.0, 0.0)
        places.append(place)
        weights.append(jnp.sum(place * gates[k], axis=1, keepdims=True))
    return (places[:window], places[window:]), (weights[:window], weights[window:])


def kernel(
    nsec, nx, nz,
    x_hbm, dy_hbm, idf_hbm, gf_hbm, idb_hbm, gb_hbm, saved_hbm, up_hbm, down_hbm,
    near, near_plr, yrecv,
    xin, ids, gates, rows, gall, gown, upw, downw, saved, ag, rs, stage, part, plr, ysend,
    load_sem, xs_send, xs_recv, gs_send, gs_recv, ag_send, ag_recv, rs_send, rs_recv,
    near_send, near_recv, y_send, y_recv, last_recv,
):
    half = nz // 2
    width = xin.shape[2]
    span = SUB * nx
    fold = width // 2
    hid = upw.shape[1] // 2
    tile = tile_of(width)
    seq = (0, 1, 3, 2) if nx == 4 else tuple(range(nx))
    back_seq = seq[::-1]
    sides = (pl.ds(0, fold), pl.ds(fold, fold))

    sec = lax.axis_index("section")
    me = lax.axis_index("expert")
    mx, mz = lax.div(me, nz), lax.rem(me, nz)
    right = (sec, mx * nz + lax.rem(mz + 1, nz))
    left = (sec, mx * nz + lax.rem(mz + nz - 1, nz))
    sec_up, sec_down = lax.rem(sec + 1, nsec), lax.rem(sec + nsec - 1, nsec)
    columns = [lax.rem(mx + i, nx) for i in range(nx)]
    targets = [lax.rem(mx + nx - i, nx) for i in range(nx)]
    out_way = (right, left)
    back_way = (left, right)

    def remote(src, dst, send, recv, device):
        return pltpu.make_async_remote_copy(
            src_ref=src, dst_ref=dst, send_sem=send, recv_sem=recv, device_id=device, device_id_type=MESH
        )

    def sub(i):
        return pl.ds(i * SUB, SUB)

    def sub_at(index):
        return pl.ds(pl.multiple_of(index * SUB, SUB), SUB)

    peers = [right, left]
    peers += [(sec, columns[i] * nz + mz) for i in range(1, nx)]
    peers += [(s, columns[i] * nz + mz) for s in (sec_up, sec_down) for i in range(nx)]
    barrier = pltpu.get_barrier_semaphore()
    for peer in peers:
        pl.semaphore_signal(barrier, inc=1, device_id=peer, device_id_type=MESH)

    loads = [
        pltpu.make_async_copy(src, dst, load_sem.at[k])
        for k, (src, dst) in enumerate((
            (idf_hbm, ids.at[0]), (gf_hbm, gates.at[0]), (idb_hbm, ids.at[1]), (gb_hbm, gates.at[1]),
            (x_hbm, xin.at[0]), (dy_hbm, xin.at[1]),
            (up_hbm, upw.at[:, pl.ds(0, hid)]), (down_hbm, downw.at[pl.ds(0, hid)]), (saved_hbm, saved),
        ))
    ]
    for load in loads:
        load.start()

    for load in loads[:4]:
        load.wait()
    places, weights = routing(ids[0], gates[0], ids[1], gates[1], nx)
    blank = jnp.zeros_like(places[0][0])
    chosen_f = jnp.concatenate([piece for e in range(nx) for piece in (places[0][e], blank)]).astype(bf16)
    chosen_b = jnp.concatenate([piece for e in range(nx) for piece in (blank, places[1][e])]).astype(bf16)
    weight = jnp.concatenate([weights[h][e] for e in range(nx) for h in range(2)])
    gall[...] = jnp.broadcast_to(weight, gall.shape)
    for load in loads[4:6]:
        load.wait()

    for step in range(width // tile):
        cols = pl.ds(step * tile, tile)
        rows[:, cols] = (
            jnp.dot(chosen_f, xin[0, :, cols], preferred_element_type=f32)
            + jnp.dot(chosen_b, xin[1, :, cols], preferred_element_type=f32)
        ).astype(bf16)

    ag[0, 0, sub(0)] = rows[sub_at(mx)]
    gown[sub(0)] = gall[sub_at(mx)]
    pl.semaphore_wait(barrier, len(peers))

    def row_copy(i, side):
        device = (sec, targets[i] * nz + mz)
        src, dst = rows.at[sub_at(targets[i]), sides[side]], ag.at[0, 0, sub(i), sides[side]]
        return remote(src, dst, xs_send.at[i - 1, side], xs_recv.at[i - 1, side], device)

    def gate_copy(i):
        device = (sec, targets[i] * nz + mz)
        return remote(
            gall.at[sub_at(targets[i])], gown.at[sub(i)], gs_send.at[i - 1], gs_recv.at[i - 1], device
        )

    def own_copy(d, i, cols):
        src, dst = ag.at[0, 0, sub(i), cols], ag.at[1, d, sub(i), cols]
        return remote(src, dst, ag_send.at[d], ag_recv.at[1, d, i], out_way[d])

    def out_copy(s, d, i):
        src, dst = ag.at[s, d, sub(i)], ag.at[s + 1, d, sub(i)]
        return remote(src, dst, ag_send.at[s + 1], ag_recv.at[s + 1, d, i], out_way[d])

    def far_copy(d, i):
        src, dst = ag.at[half - 1, d, sub(i), sides[d]], ag.at[0, 1, sub(i), sides[d]]
        return remote(src, dst, ag_send.at[half + d], ag_recv.at[0, d, i], out_way[d])

    for d in range(2):
        own_copy(d, 0, pl.ds(0, width)).start()
    pieces = [(i, side) for group in (seq[1:3], seq[3:]) for side in range(2) for i in group]
    for i, side in pieces:
        row_copy(i, side).start()
    for i in range(1, nx):
        gate_copy(i).start()

    next_of = ((sec_up, me), (sec_down, me))
    near_copies = [
        remote(src.at[h], dst.at[h], near_send.at[h, k], near_recv.at[h, k], next_of[h])
        for h in range(2)
        for k, (src, dst) in enumerate(((xin, near), (plr, near_plr)))
    ]
    near_copies[0].start()
    near_copies[2].start()

    for i, side in pieces:
        row_copy(i, side).wait_recv()
        for d in range(2):
            own_copy(d, i, sides[side]).start()

    for load in loads[6:]:
        load.wait()

    @pl.loop(0, width // tile)
    def _(step):
        cols = pl.ds(pl.multiple_of(step * tile, tile), tile)
        upw[cols, pl.ds(hid, hid)] = downw[pl.ds(0, hid), cols].T
        downw[pl.ds(hid, hid), cols] = upw[cols, pl.ds(0, hid)].T

    @pl.loop(0, nx)
    def _(column):
        value = saved[column]
        sig = jax.nn.sigmoid(value)
        saved[column] = sig * (1.0 + value * (1.0 - sig))

    for h in range(2):
        pairs = [[places[h][e], blank] for e in range(nx)] + [[blank, places[h][e]] for e in range(nx)]
        spots = jnp.concatenate([piece for pair in pairs for piece in pair])
        plr[h] = spots.T.astype(bf16)
        near_copies[2 * h + 1].start()

    def compute(s, first, sources):
        count = len(sources)
        blocks = pl.ds(first, count)

        def add_up(step, total):
            cols = pl.ds(pl.multiple_of(step * tile, tile), tile)
            block = ag[s, blocks, :, cols].reshape(count * span, tile)
            return total + jnp.dot(block, upw[cols, :], preferred_element_type=f32)

        total = lax.fori_loop(0, width // tile, add_up, jnp.zeros((count * span, 2 * hid), f32))
        total = total.reshape(count * nx, 2, CAP, 2 * hid)
        forward = total[:, 0, :, :hid]
        forward = forward * jax.nn.sigmoid(forward)
        slope = jnp.stack([saved[columns[i], source] for source in sources for i in range(nx)])
        backward = total[:, 1, :, hid:] * slope
        none = jnp.zeros_like(forward)
        inner = jnp.stack(
            [jnp.concatenate([forward, none], axis=-1), jnp.concatenate([none, backward], axis=-1)], axis=1
        )
        inner = inner.reshape(count * span, 2 * hid).astype(bf16)

        @pl.loop(0, width // tile)
        def _(step):
            cols = pl.ds(pl.multiple_of(step * tile, tile), tile)
            result = jnp.dot(inner, downw[:, cols], preferred_element_type=f32)
            part[s, blocks, :, cols] = result.reshape(count, span, tile)

    def both(s):
        return (lax.rem(mz + nz - s, nz), lax.rem(mz + s, nz))

    @pl.loop(1, half - 1)
    def _(s):
        for i in seq:
            for d in range(2):
                out_copy(s - 1, d, i).wait_recv()
                out_copy(s, d, i).start()
        compute(s, 0, both(s))

    for i in seq:
        for d in range(2):
            out_copy(half - 2, d, i).wait_recv()
            far_copy(d, i).start()
    compute(half - 1, 0, both(half - 1))

    def back_copy(s, d, i):
        return remote(
            rs.at[s, d, sub(i)], rs.at[s - 1, d, sub(i)], rs_send.at[s], rs_recv.at[s - 1, d, i], back_way[d]
        )

    def half_copy(d, i, side):
        src, dst = rs.at[half - 1, d, sub(i), sides[side]], rs.at[half - 2, d, sub(i), sides[side]]
        return remote(src, dst, rs_send.at[half - 1], rs_recv.at[half - 2, d, i], back_way[d])

    def first_copy(d, i):
        src, dst = stage.at[sub(i), sides[d]], rs.at[half - 1, d, sub(i), sides[d]]
        return remote(src, dst, rs_send.at[0], rs_recv.at[half - 1, d, i], back_way[d])

    for i in back_seq:
        for d in range(2):
            cols = sides[1 - d]
            rs[half - 1, d, sub(i), cols] = part[half - 1, d, sub(i), cols].astype(bf16)
            half_copy(d, i, 1 - d).start()
    for i in seq:
        for d in range(2):
            far_copy(d, i).wait_recv()
    compute(0, 1, (lax.rem(mz + half, nz),))
    for i in back_seq:
        stage[sub(i)] = part[0, 1, sub(i)].astype(bf16)
        for d in range(2):
            first_copy(d, i).start()
    compute(0, 0, (mz,))
    for i in back_seq:
        for d in range(2):
            cols = sides[d]
            first_copy(d, i).wait_recv()
            here = rs[half - 1, d, sub(i), cols].astype(f32) + part[half - 1, d, sub(i), cols]
            rs[half - 1, d, sub(i), cols] = here.astype(bf16)
            half_copy(d, i, d).start()

    @pl.loop(1, half - 2)
    def _(step):
        s = half - 1 - step
        for i in back_seq:
            for d in range(2):
                back_copy(s + 1, d, i).wait_recv()
                rs[s, d, sub(i)] = (rs[s, d, sub(i)].astype(f32) + part[s, d, sub(i)]).astype(bf16)
                back_copy(s, d, i).start()
        remote(ag.at[s], ag.at[s], ag_send.at[s + 1], ag_recv.at[s, 0, 0], right).wait_send()

    def last_copy(d, i, side):
        src, dst = rs.at[1, d, sub(i), sides[side]], rs.at[0, d, sub(i), sides[side]]
        return remote(src, dst, rs_send.at[1], last_recv.at[d, i, side], back_way[d])

    for i in back_seq:
        for d in range(2):
            back_copy(2, d, i).wait_recv()
        for side in range(2):
            for d in range(2):
                here = rs[1, d, sub(i), sides[side]].astype(f32) + part[1, d, sub(i), sides[side]]
                rs[1, d, sub(i), sides[side]] = here.astype(bf16)
                last_copy(d, i, side).start()
    remote(ag.at[1], ag.at[1], ag_send.at[2], ag_recv.at[1, 0, 0], right).wait_send()

    for i in range(1, nx):
        gate_copy(i).wait_recv()

    quarter = fold // 2

    def y_copy(h, i, side):
        device = ((sec_up, sec_down)[h], columns[i] * nz + mz)
        cols = pl.ds(side * quarter, quarter)
        src, dst = ysend.at[h, sub(i), cols], yrecv.at[h, sub_at(mx), cols]
        return remote(src, dst, y_send.at[h], y_recv.at[h, mx], device)

    for i in back_seq:
        gate = gown[sub(i), 0:1]
        for side in range(2):
            for d in range(2):
                last_copy(d, i, side).wait_recv()
            total = part[0, 0, sub(i), sides[side]]
            for d in range(2):
                total = total + rs[0, d, sub(i), sides[side]].astype(f32)
            value = ag[0, 0, sub(i), sides[side]].astype(f32) + gate * total
            for h in range(2):
                picked = value[h * CAP : (h + 1) * CAP]
                folded = jnp.concatenate([picked[:, :quarter], picked[:, quarter:]], axis=0)
                ysend[h, sub(i), pl.ds(side * quarter, quarter)] = folded.astype(bf16)
                y_copy(h, i, side).start()

    for copy in near_copies:
        copy.wait()
    for h in range(2):
        for e in range(nx):
            remote(ysend.at[h, sub(e)], yrecv.at[h, sub(e)], y_send.at[h], y_recv.at[h, e], next_of[h]).wait_recv()

    for i in range(1, nx):
        for side in range(2):
            row_copy(i, side).wait_send()
        gate_copy(i).wait_send()
    for d in range(2):
        remote(ag.at[0, 0], ag.at[1, d], ag_send.at[d], ag_recv.at[1, d, 0], right).wait_send()
        far = ag.at[half - 1, d, :, sides[d]]
        remote(far, far, ag_send.at[half + d], ag_recv.at[0, 1, 0], right).wait_send()
        remote(ysend.at[d], yrecv.at[d], y_send.at[d], y_recv.at[d, 0], right).wait_send()
    remote(stage, rs.at[0, 0], rs_send.at[0], rs_recv.at[0, 0, 0], right).wait_send()
    for s in range(1, half):
        remote(rs.at[s], rs.at[s - 1], rs_send.at[s], rs_recv.at[0, 0, 0], right).wait_send()

def place_rows(near, places, moved, outf, outb, done, out_sem):
    width = near.shape[2]
    fold = width // 2
    span = moved.shape[1]
    stores = []
    quarter = fold // 2
    for h in range(2):
        place = places[h]
        with_share = jnp.max(place.astype(f32), axis=1, keepdims=True) > 0.5
        for side in range(2):
            share = moved[h, :, side * quarter : (side + 1) * quarter]
            for k in range(2):
                cols = pl.ds((2 * side + k) * quarter, quarter)
                spots = place[:, k * span : (k + 1) * span]
                here = jnp.dot(spots, share, preferred_element_type=f32)
                done[h, :, cols] = jnp.where(with_share, here, near[h, :, cols].astype(f32)).astype(bf16)
            cols = pl.ds(side * fold, fold)
            store = pltpu.make_async_copy(done.at[h, :, cols], (outf, outb)[h].at[:, cols], out_sem.at[h, side])
            store.start()
            stores.append(store)
    for store in stores:
        store.wait()


def per_device(x_fwd, ids_fwd, gates_fwd, dy_bwd, ids_bwd, gates_bwd, saved_hidden, w_up, w_down):
    nsec = lax.axis_size("section")
    devices = lax.axis_size("expert")
    hid = w_up.shape[2]
    nz = FF // hid
    nx = devices // nz
    half = nz // 2
    tokens, width = x_fwd.shape[1:]
    span = SUB * nx
    choices = ids_fwd.shape[2]
    any_space = pl.BlockSpec(memory_space=pl.ANY)
    vmem = pl.BlockSpec(memory_space=pltpu.VMEM)
    dma = pltpu.SemaphoreType.DMA
    near, near_plr, yrecv = pl.pallas_call(
        functools.partial(kernel, nsec, nx, nz),
        out_shape=[
            pltpu.VMEM((2, tokens, width), bf16),
            pltpu.VMEM((2, tokens, 2 * span), bf16),
            pltpu.VMEM((2, span, width // 2), bf16),
        ],
        in_specs=[any_space] * 9,
        out_specs=[vmem] * 3,
        scratch_shapes=[
            pltpu.VMEM((2, tokens, width), bf16),
            pltpu.VMEM((2, choices, tokens), jnp.int32),
            pltpu.VMEM((2, choices, tokens), f32),
            pltpu.VMEM((span, width), bf16),
            pltpu.VMEM((span, 128), f32),
            pltpu.VMEM((span, 128), f32),
            pltpu.VMEM((width, 2 * hid), bf16),
            pltpu.VMEM((2 * hid, width), bf16),
            pltpu.VMEM((nx, nz, CAP, hid), f32),
            pltpu.VMEM((half, 2, span, width), bf16),
            pltpu.VMEM((half, 2, span, width), bf16),
            pltpu.VMEM((span, width), bf16),
            pltpu.VMEM((half, 2, span, width), f32),
            pltpu.VMEM((2, tokens, 2 * span), bf16),
            pltpu.VMEM((2, span, width // 2), bf16),
            dma((9,)),
            dma((nx - 1, 2)), dma((nx - 1, 2)), dma((nx - 1,)), dma((nx - 1,)),
            dma((half + 2,)), dma((half, 2, nx)),
            dma((half,)), dma((half, 2, nx)),
            dma((2, 2)), dma((2, 2)), dma((2,)), dma((2, nx)), dma((2, nx, 2)),
        ],
        compiler_params=pltpu.CompilerParams(
            collective_id=0, has_side_effects=True, vmem_limit_bytes=56 * 1024 * 1024
        ),
    )(
        x_fwd[0], dy_bwd[0], ids_fwd[0].T, gates_fwd[0].T, ids_bwd[0].T, gates_bwd[0].T,
        saved_hidden[0].reshape(nx, nz, CAP, hid), w_up[0], w_down[0],
    )
    outs = pl.pallas_call(
        place_rows,
        out_shape=[jax.ShapeDtypeStruct((tokens, width), bf16)] * 2,
        in_specs=[vmem] * 3,
        out_specs=[any_space] * 2,
        scratch_shapes=[pltpu.VMEM((2, tokens, width), bf16), dma((2, 2))],
        compiler_params=pltpu.CompilerParams(vmem_limit_bytes=32 * 1024 * 1024),
    )(*(pltpu.with_memory_space_constraint(v, pltpu.VMEM) for v in (near, near_plr, yrecv)))
    return (outs[0][None], outs[1][None])


def solution(mesh):
    in_specs = (
        P("section", "expert", None),
        P("section", "expert", None),
        P("section", "expert", None),
        P("section", "expert", None),
        P("section", "expert", None),
        P("section", "expert", None),
        P("section", None, "expert"),
        P("section", None, "expert"),
        P("section", "expert", None),
    )
    out_specs = (P("section", "expert", None), P("section", "expert", None))
    return jax.shard_map(
        per_device, mesh=mesh, in_specs=in_specs, out_specs=out_specs, check_vma=False
    )
```

```python
import functools
import math

import jax
import jax.numpy as jnp
from jax import lax
from jax.experimental import pallas as pl
from jax.experimental.pallas import tpu as pltpu
from jax.sharding import PartitionSpec as P

MESH = pl.DeviceIdType.MESH
CAP = 8
SUB = 2 * CAP
FF = 2048
TOP_CODE = 32000.0
LEVELS = 256 / math.log(2)
f32 = jnp.float32
bf16 = jnp.bfloat16
i32 = jnp.int32
i16 = jnp.int16


def tile_of(width):
    return 512 if width % 512 == 0 else 128


def routing(ids_f, gates_f, ids_b, gates_b, window):
    rows = ids_f.shape[1]
    routed, gates = [], []
    for ids, values in ((ids_f, gates_f), (ids_b, gates_b)):
        for e in range(window):
            match = ids == e
            routed.append(jnp.max(jnp.where(match, 1.0, 0.0), axis=0, keepdims=True))
            gates.append(jnp.sum(jnp.where(match, values, 0.0), axis=0, keepdims=True))
    earlier = lax.broadcasted_iota(i32, (rows, rows), 0) < lax.broadcasted_iota(
        i32, (rows, rows), 1
    )
    position = jnp.dot(
        jnp.concatenate(routed, axis=0).astype(bf16),
        jnp.where(earlier, 1.0, 0.0).astype(bf16),
        preferred_element_type=f32,
    )
    slot = lax.broadcasted_iota(i32, (CAP, rows), 0).astype(f32)
    places, weights = [], []
    for k in range(2 * window):
        place = jnp.where((position[k : k + 1] == slot) & (routed[k] > 0.5), 1.0, 0.0)
        places.append(place)
        weights.append(jnp.sum(place * gates[k], axis=1, keepdims=True))
    return (places[:window], places[window:]), (weights[:window], weights[window:])


def kernel(
    nsec, nx, nz,
    x_hbm, dy_hbm, idf_hbm, gf_hbm, idb_hbm, gb_hbm, saved_hbm, up_hbm, down_hbm,
    near, near_plr, yrecv,
    xin, ids, gates, rows, gall, gown, upw, downw, saved, ag, rs, stage, part, plr, ysend,
    load_sem, xs_send, xs_recv, gs_send, gs_recv, ag_send, ag_recv, rs_send, rs_recv,
    near_send, near_recv, y_send, y_recv, last_recv,
):
    half = nz // 2
    width = xin.shape[2]
    span = SUB * nx
    fold = width // 2
    hid = upw.shape[1] // 2
    tile = tile_of(width)
    seq = (0, 1, 3, 2) if nx == 4 else tuple(range(nx))
    back_seq = seq[::-1]
    sides = (pl.ds(0, fold), pl.ds(fold, fold))
    code_cols = (pl.ds(0, fold), pl.ds(fold + 128, fold))
    level_cols = (pl.ds(fold, 128), pl.ds(width + 128, 128))
    wire_sides = (pl.ds(0, fold + 128), pl.ds(fold + 128, fold + 128))
    wire_whole = pl.ds(0, width + 128)

    sec = lax.axis_index("section")
    me = lax.axis_index("expert")
    mx, mz = lax.div(me, nz), lax.rem(me, nz)
    right = (sec, mx * nz + lax.rem(mz + 1, nz))
    left = (sec, mx * nz + lax.rem(mz + nz - 1, nz))
    sec_up, sec_down = lax.rem(sec + 1, nsec), lax.rem(sec + nsec - 1, nsec)
    columns = [lax.rem(mx + i, nx) for i in range(nx)]
    targets = [lax.rem(mx + nx - i, nx) for i in range(nx)]
    out_way = (right, left)
    back_way = (left, right)

    def remote(src, dst, send, recv, device):
        return pltpu.make_async_remote_copy(
            src_ref=src, dst_ref=dst, send_sem=send, recv_sem=recv, device_id=device, device_id_type=MESH
        )

    def sub(i):
        return pl.ds(i * SUB, SUB)

    def sub_at(index):
        return pl.ds(pl.multiple_of(index * SUB, SUB), SUB)

    peers = [right, left]
    peers += [(sec, columns[i] * nz + mz) for i in range(1, nx)]
    peers += [(s, columns[i] * nz + mz) for s in (sec_up, sec_down) for i in range(nx)]
    barrier = pltpu.get_barrier_semaphore()
    for peer in peers:
        pl.semaphore_signal(barrier, inc=1, device_id=peer, device_id_type=MESH)

    loads = [
        pltpu.make_async_copy(src, dst, load_sem.at[k])
        for k, (src, dst) in enumerate((
            (idf_hbm, ids.at[0]), (gf_hbm, gates.at[0]), (idb_hbm, ids.at[1]), (gb_hbm, gates.at[1]),
            (x_hbm, xin.at[0]), (dy_hbm, xin.at[1]),
            (up_hbm, upw.at[:, pl.ds(0, hid)]), (down_hbm, downw.at[pl.ds(0, hid)]), (saved_hbm, saved),
        ))
    ]
    for load in loads:
        load.start()

    for load in loads[:4]:
        load.wait()
    places, weights = routing(ids[0], gates[0], ids[1], gates[1], nx)
    blank = jnp.zeros_like(places[0][0])
    chosen_f = jnp.concatenate([piece for e in range(nx) for piece in (places[0][e], blank)]).astype(bf16)
    chosen_b = jnp.concatenate([piece for e in range(nx) for piece in (blank, places[1][e])]).astype(bf16)
    weight = jnp.concatenate([weights[h][e] for e in range(nx) for h in range(2)])
    gall[...] = jnp.broadcast_to(weight, gall.shape)
    for load in loads[4:6]:
        load.wait()

    for step in range(width // tile):
        cols = pl.ds(step * tile, tile)
        rows[:, cols] = (
            jnp.dot(chosen_f, xin[0, :, cols], preferred_element_type=f32)
            + jnp.dot(chosen_b, xin[1, :, cols], preferred_element_type=f32)
        ).astype(bf16)

    ag[0, 0, sub(0)] = rows[sub_at(mx)]
    gown[sub(0)] = gall[sub_at(mx)]
    pl.semaphore_wait(barrier, len(peers))

    def row_copy(i, side):
        device = (sec, targets[i] * nz + mz)
        src, dst = rows.at[sub_at(targets[i]), sides[side]], ag.at[0, 0, sub(i), sides[side]]
        return remote(src, dst, xs_send.at[i - 1, side], xs_recv.at[i - 1, side], device)

    def gate_copy(i):
        device = (sec, targets[i] * nz + mz)
        return remote(
            gall.at[sub_at(targets[i])], gown.at[sub(i)], gs_send.at[i - 1], gs_recv.at[i - 1], device
        )

    def own_copy(d, i, cols):
        src, dst = ag.at[0, 0, sub(i), cols], ag.at[1, d, sub(i), cols]
        return remote(src, dst, ag_send.at[d], ag_recv.at[1, d, i], out_way[d])

    def out_copy(s, d, i):
        src, dst = ag.at[s, d, sub(i)], ag.at[s + 1, d, sub(i)]
        return remote(src, dst, ag_send.at[s + 1], ag_recv.at[s + 1, d, i], out_way[d])

    def far_copy(d, i):
        src, dst = ag.at[half - 1, d, sub(i), sides[d]], ag.at[0, 1, sub(i), sides[d]]
        return remote(src, dst, ag_send.at[half + d], ag_recv.at[0, d, i], out_way[d])

    for d in range(2):
        own_copy(d, 0, pl.ds(0, width)).start()
    pieces = [(i, side) for group in (seq[1:3], seq[3:]) for side in range(2) for i in group]
    for i, side in pieces:
        row_copy(i, side).start()
    for i in range(1, nx):
        gate_copy(i).start()

    next_of = ((sec_up, me), (sec_down, me))
    near_copies = [
        remote(src.at[h], dst.at[h], near_send.at[h, k], near_recv.at[h, k], next_of[h])
        for h in range(2)
        for k, (src, dst) in enumerate(((xin, near), (plr, near_plr)))
    ]
    near_copies[0].start()
    near_copies[2].start()

    for i, side in pieces:
        row_copy(i, side).wait_recv()
        for d in range(2):
            own_copy(d, i, sides[side]).start()

    for load in loads[6:]:
        load.wait()

    @pl.loop(0, width // tile)
    def _(step):
        cols = pl.ds(pl.multiple_of(step * tile, tile), tile)
        upw[cols, pl.ds(hid, hid)] = downw[pl.ds(0, hid), cols].T
        downw[pl.ds(hid, hid), cols] = upw[cols, pl.ds(0, hid)].T

    @pl.loop(0, nx)
    def _(column):
        value = saved[column]
        sig = jax.nn.sigmoid(value)
        saved[column] = sig * (1.0 + value * (1.0 - sig))

    for h in range(2):
        pairs = [[places[h][e], blank] for e in range(nx)] + [[blank, places[h][e]] for e in range(nx)]
        spots = jnp.concatenate([piece for pair in pairs for piece in pair])
        plr[h] = spots.T.astype(bf16)
        near_copies[2 * h + 1].start()

    def compute(s, first, sources):
        count = len(sources)
        blocks = pl.ds(first, count)

        def add_up(step, total):
            cols = pl.ds(pl.multiple_of(step * tile, tile), tile)
            block = ag[s, blocks, :, cols].reshape(count * span, tile)
            return total + jnp.dot(block, upw[cols, :], preferred_element_type=f32)

        total = lax.fori_loop(0, width // tile, add_up, jnp.zeros((count * span, 2 * hid), f32))
        total = total.reshape(count * nx, 2, CAP, 2 * hid)
        forward = total[:, 0, :, :hid]
        forward = forward * jax.nn.sigmoid(forward)
        slope = jnp.stack([saved[columns[i], source] for source in sources for i in range(nx)])
        backward = total[:, 1, :, hid:] * slope
        none = jnp.zeros_like(forward)
        inner = jnp.stack(
            [jnp.concatenate([forward, none], axis=-1), jnp.concatenate([none, backward], axis=-1)], axis=1
        )
        inner = inner.reshape(count * span, 2 * hid).astype(bf16)

        @pl.loop(0, width // tile)
        def _(step):
            cols = pl.ds(pl.multiple_of(step * tile, tile), tile)
            result = jnp.dot(inner, downw[:, cols], preferred_element_type=f32)
            part[s, blocks, :, cols] = result.reshape(count, span, tile).astype(bf16)

    def both(s):
        return (lax.rem(mz + nz - s, nz), lax.rem(mz + s, nz))

    @pl.loop(1, half - 1)
    def _(s):
        for i in seq:
            for d in range(2):
                out_copy(s - 1, d, i).wait_recv()
                out_copy(s, d, i).start()
        compute(s, 0, both(s))

    for i in seq:
        for d in range(2):
            out_copy(half - 2, d, i).wait_recv()
            far_copy(d, i).start()
    compute(half - 1, 0, both(half - 1))

    def top_of(value):
        return jnp.max(jnp.abs(value), axis=1, keepdims=True)

    def level_of(top):
        return jnp.ceil(jnp.log(jnp.maximum(top, 1e-30) * (1.0 / TOP_CODE)) * LEVELS)

    def write(ref, i, side, value, level):
        codes = jnp.round(value * jnp.exp(level * (-1.0 / LEVELS)))
        ref[sub(i), code_cols[side]] = codes.astype(i32).astype(i16)

    def mark(ref, i, side, level):
        ref[sub(i), level_cols[side]] = jnp.broadcast_to(level, (SUB, 128)).astype(i32).astype(i16)

    def write_half(ref, i, side, value):
        level = level_of(top_of(value))
        write(ref, i, side, value, level)
        mark(ref, i, side, level)

    def write_whole(ref, i, values):
        level = level_of(jnp.maximum(top_of(values[0]), top_of(values[1])))
        for side in range(2):
            write(ref, i, side, values[side], level)
        mark(ref, i, 0, level)

    def read(ref, i, side, mark_side):
        level = ref[sub(i), level_cols[mark_side]].astype(i32).astype(f32)[:, :1]
        return ref[sub(i), code_cols[side]].astype(i32).astype(f32) * jnp.exp(level * (1.0 / LEVELS))

    def term(s, d, i, side):
        return part[s, d, sub(i), sides[side]].astype(f32)

    def back_copy(s, d, i):
        src, dst = rs.at[s, d, sub(i), wire_whole], rs.at[s - 1, d, sub(i), wire_whole]
        return remote(src, dst, rs_send.at[s], rs_recv.at[s - 1, d, i], back_way[d])

    def half_copy(d, i, side):
        src, dst = rs.at[half - 1, d, sub(i), wire_sides[side]], rs.at[half - 2, d, sub(i), wire_sides[side]]
        return remote(src, dst, rs_send.at[half - 1], rs_recv.at[half - 2, d, i], back_way[d])

    def both_halves(d, i):
        src, dst = rs.at[half - 1, d, sub(i)], rs.at[half - 2, d, sub(i)]
        return remote(src, dst, rs_send.at[half - 1], rs_recv.at[half - 2, d, i], back_way[d])

    def first_copy(d, i):
        src, dst = stage.at[sub(i), wire_sides[d]], rs.at[half - 1, d, sub(i), wire_sides[d]]
        return remote(src, dst, rs_send.at[0], rs_recv.at[half - 1, d, i], back_way[d])

    def last_copy(d, i, side):
        src, dst = rs.at[1, d, sub(i), wire_sides[side]], rs.at[0, d, sub(i), wire_sides[side]]
        return remote(src, dst, rs_send.at[1], last_recv.at[d, i, side], back_way[d])

    for i in back_seq:
        for d in range(2):
            write_half(rs.at[half - 1, d], i, 1 - d, term(half - 1, d, i, 1 - d))
            half_copy(d, i, 1 - d).start()
    for i in seq:
        for d in range(2):
            far_copy(d, i).wait_recv()
    compute(0, 1, (lax.rem(mz + half, nz),))
    for i in back_seq:
        for d in range(2):
            write_half(stage, i, d, term(0, 1, i, d))
            first_copy(d, i).start()
    compute(0, 0, (mz,))
    for i in back_seq:
        for d in range(2):
            first_copy(d, i).wait_recv()
            ref = rs.at[half - 1, d]
            write_half(ref, i, d, read(ref, i, d, d) + term(half - 1, d, i, d))
            half_copy(d, i, d).start()

    def pass_on(s, d, i, marks):
        ref = rs.at[s, d]
        write_whole(ref, i, [read(ref, i, side, marks[side]) + term(s, d, i, side) for side in range(2)])
        back_copy(s, d, i).start()

    def settle(s):
        remote(ag.at[s], ag.at[s], ag_send.at[s + 1], ag_recv.at[s, 0, 0], right).wait_send()

    for i in back_seq:
        for d in range(2):
            both_halves(d, i).wait_recv()
            pass_on(half - 2, d, i, (0, 1))
    settle(half - 2)

    @pl.loop(1, half - 3)
    def _(step):
        s = half - 2 - step
        for i in back_seq:
            for d in range(2):
                back_copy(s + 1, d, i).wait_recv()
                pass_on(s, d, i, (0, 0))
        settle(s)

    for i in back_seq:
        for d in range(2):
            back_copy(2, d, i).wait_recv()
        sums = [[read(rs.at[1, d], i, side, 0) + term(1, d, i, side) for d in range(2)] for side in range(2)]
        for side in range(2):
            for d in range(2):
                write_half(rs.at[1, d], i, side, sums[side][d])
                last_copy(d, i, side).start()
    settle(1)

    for i in range(1, nx):
        gate_copy(i).wait_recv()

    quarter = fold // 2

    def y_copy(h, i, side):
        device = ((sec_up, sec_down)[h], columns[i] * nz + mz)
        cols = pl.ds(side * quarter, quarter)
        src, dst = ysend.at[h, sub(i), cols], yrecv.at[h, sub_at(mx), cols]
        return remote(src, dst, y_send.at[h], y_recv.at[h, mx], device)

    for i in range(1, nx):
        for side in range(2):
            row_copy(i, side).wait_send()
        gate_copy(i).wait_send()
    for d in range(2):
        remote(ag.at[0, 0], ag.at[1, d], ag_send.at[d], ag_recv.at[1, d, 0], right).wait_send()
        far = ag.at[half - 1, d, :, sides[d]]
        remote(far, far, ag_send.at[half + d], ag_recv.at[0, 1, 0], right).wait_send()
    remote(stage, rs.at[0, 0], rs_send.at[0], rs_recv.at[0, 0, 0], right).wait_send()
    for s in range(2, half):
        sent = rs.at[s, :, :, wire_whole] if s < half - 1 else rs.at[s]
        remote(sent, sent, rs_send.at[s], rs_recv.at[0, 0, 0], right).wait_send()
    for copy in near_copies:
        copy.wait()

    for i in back_seq:
        gate = gown[sub(i), 0:1]
        for side in range(2):
            for d in range(2):
                last_copy(d, i, side).wait_recv()
            total = term(0, 0, i, side)
            for d in range(2):
                total = total + read(rs.at[0, d], i, side, side)
            value = ag[0, 0, sub(i), sides[side]].astype(f32) + gate * total
            for h in range(2):
                picked = value[h * CAP : (h + 1) * CAP]
                folded = jnp.concatenate([picked[:, :quarter], picked[:, quarter:]], axis=0)
                ysend[h, sub(i), pl.ds(side * quarter, quarter)] = folded.astype(bf16)
                y_copy(h, i, side).start()

    for h in range(2):
        for e in range(nx):
            remote(ysend.at[h, sub(e)], yrecv.at[h, sub(e)], y_send.at[h], y_recv.at[h, e], next_of[h]).wait_recv()

    for d in range(2):
        remote(ysend.at[d], yrecv.at[d], y_send.at[d], y_recv.at[d, 0], right).wait_send()
    remote(rs.at[1], rs.at[0], rs_send.at[1], rs_recv.at[0, 0, 0], right).wait_send()


def place_rows(near, places, moved, outf, outb, done, out_sem):
    width = near.shape[2]
    fold = width // 2
    span = moved.shape[1]
    stores = []
    quarter = fold // 2
    for h in range(2):
        place = places[h]
        with_share = jnp.max(place.astype(f32), axis=1, keepdims=True) > 0.5
        for side in range(2):
            share = moved[h, :, side * quarter : (side + 1) * quarter]
            for k in range(2):
                cols = pl.ds((2 * side + k) * quarter, quarter)
                spots = place[:, k * span : (k + 1) * span]
                here = jnp.dot(spots, share, preferred_element_type=f32)
                done[h, :, cols] = jnp.where(with_share, here, near[h, :, cols].astype(f32)).astype(bf16)
            cols = pl.ds(side * fold, fold)
            store = pltpu.make_async_copy(done.at[h, :, cols], (outf, outb)[h].at[:, cols], out_sem.at[h, side])
            store.start()
            stores.append(store)
    for store in stores:
        store.wait()


def per_device(x_fwd, ids_fwd, gates_fwd, dy_bwd, ids_bwd, gates_bwd, saved_hidden, w_up, w_down):
    nsec = lax.axis_size("section")
    devices = lax.axis_size("expert")
    hid = w_up.shape[2]
    nz = FF // hid
    nx = devices // nz
    half = nz // 2
    tokens, width = x_fwd.shape[1:]
    span = SUB * nx
    choices = ids_fwd.shape[2]
    any_space = pl.BlockSpec(memory_space=pl.ANY)
    vmem = pl.BlockSpec(memory_space=pltpu.VMEM)
    dma = pltpu.SemaphoreType.DMA
    near, near_plr, yrecv = pl.pallas_call(
        functools.partial(kernel, nsec, nx, nz),
        out_shape=[
            pltpu.VMEM((2, tokens, width), bf16),
            pltpu.VMEM((2, tokens, 2 * span), bf16),
            pltpu.VMEM((2, span, width // 2), bf16),
        ],
        in_specs=[any_space] * 9,
        out_specs=[vmem] * 3,
        scratch_shapes=[
            pltpu.VMEM((2, tokens, width), bf16),
            pltpu.VMEM((2, choices, tokens), i32),
            pltpu.VMEM((2, choices, tokens), f32),
            pltpu.VMEM((span, width), bf16),
            pltpu.VMEM((span, 128), f32),
            pltpu.VMEM((span, 128), f32),
            pltpu.VMEM((width, 2 * hid), bf16),
            pltpu.VMEM((2 * hid, width), bf16),
            pltpu.VMEM((nx, nz, CAP, hid), f32),
            pltpu.VMEM((half, 2, span, width), bf16),
            pltpu.VMEM((half, 2, span, width + 256), i16),
            pltpu.VMEM((span, width + 256), i16),
            pltpu.VMEM((half, 2, span, width), bf16),
            pltpu.VMEM((2, tokens, 2 * span), bf16),
            pltpu.VMEM((2, span, width // 2), bf16),
            dma((9,)),
            dma((nx - 1, 2)), dma((nx - 1, 2)), dma((nx - 1,)), dma((nx - 1,)),
            dma((half + 2,)), dma((half, 2, nx)),
            dma((half,)), dma((half, 2, nx)),
            dma((2, 2)), dma((2, 2)), dma((2,)), dma((2, nx)), dma((2, nx, 2)),
        ],
        compiler_params=pltpu.CompilerParams(
            collective_id=0, has_side_effects=True, vmem_limit_bytes=56 * 1024 * 1024
        ),
    )(
        x_fwd[0], dy_bwd[0], ids_fwd[0].T, gates_fwd[0].T, ids_bwd[0].T, gates_bwd[0].T,
        saved_hidden[0].reshape(nx, nz, CAP, hid), w_up[0], w_down[0],
    )
    outs = pl.pallas_call(
        place_rows,
        out_shape=[jax.ShapeDtypeStruct((tokens, width), bf16)] * 2,
        in_specs=[vmem] * 3,
        out_specs=[any_space] * 2,
        scratch_shapes=[pltpu.VMEM((2, tokens, width), bf16), dma((2, 2))],
        compiler_params=pltpu.CompilerParams(vmem_limit_bytes=32 * 1024 * 1024),
    )(*(pltpu.with_memory_space_constraint(v, pltpu.VMEM) for v in (near, near_plr, yrecv)))
    return (outs[0][None], outs[1][None])


def solution(mesh):
    in_specs = (
        P("section", "expert", None),
        P("section", "expert", None),
        P("section", "expert", None),
        P("section", "expert", None),
        P("section", "expert", None),
        P("section", "expert", None),
        P("section", None, "expert"),
        P("section", None, "expert"),
        P("section", "expert", None),
    )
    out_specs = (P("section", "expert", None), P("section", "expert", None))
    return jax.shard_map(
        per_device, mesh=mesh, in_specs=in_specs, out_specs=out_specs, check_vma=False
    )
```

```python
import functools
import math

import jax
import jax.numpy as jnp
from jax import lax
from jax.experimental import pallas as pl
from jax.experimental.pallas import tpu as pltpu
from jax.sharding import PartitionSpec as P

MESH = pl.DeviceIdType.MESH
CAP = 8
SUB = 2 * CAP
FF = 2048
TOP_CODE = 32000.0
LEVELS = 256 / math.log(2)
f32 = jnp.float32
bf16 = jnp.bfloat16
i32 = jnp.int32
i16 = jnp.int16


def tile_of(width):
    return 512 if width % 512 == 0 else 128


def routing(ids_f, gates_f, ids_b, gates_b, window):
    rows = ids_f.shape[1]
    routed, gates = [], []
    for ids, values in ((ids_f, gates_f), (ids_b, gates_b)):
        for e in range(window):
            match = ids == e
            routed.append(jnp.max(jnp.where(match, 1.0, 0.0), axis=0, keepdims=True))
            gates.append(jnp.sum(jnp.where(match, values, 0.0), axis=0, keepdims=True))
    earlier = lax.broadcasted_iota(i32, (rows, rows), 0) < lax.broadcasted_iota(
        i32, (rows, rows), 1
    )
    position = jnp.dot(
        jnp.concatenate(routed, axis=0).astype(bf16),
        jnp.where(earlier, 1.0, 0.0).astype(bf16),
        preferred_element_type=f32,
    )
    slot = lax.broadcasted_iota(i32, (CAP, rows), 0).astype(f32)
    places, weights = [], []
    for k in range(2 * window):
        place = jnp.where((position[k : k + 1] == slot) & (routed[k] > 0.5), 1.0, 0.0)
        places.append(place)
        weights.append(jnp.sum(place * gates[k], axis=1, keepdims=True))
    return (places[:window], places[window:]), (weights[:window], weights[window:])


def kernel(
    nsec, nx, nz,
    x_hbm, dy_hbm, idf_hbm, gf_hbm, idb_hbm, gb_hbm, saved_hbm, up_hbm, down_hbm,
    near, near_plr, yrecv,
    level_in, level_out, bound,
    xin, ids, gates, rows, gall, gown, upw, downw, saved, ag, rs, stage, part, plr, ysend,
    load_sem, xs_send, xs_recv, gs_send, gs_recv, ag_send, ag_recv, rs_send, rs_recv,
    near_send, near_recv, y_send, y_recv, last_recv, lv_send, lv_recv,
):
    half = nz // 2
    width = xin.shape[2]
    span = SUB * nx
    fold = width // 2
    hid = upw.shape[1] // 2
    tile = tile_of(width)
    seq = (0, 1, 3, 2) if nx == 4 else tuple(range(nx))
    back_seq = seq[::-1]
    sides = (pl.ds(0, fold), pl.ds(fold, fold))
    group = 128 // nx

    sec = lax.axis_index("section")
    me = lax.axis_index("expert")
    mx, mz = lax.div(me, nz), lax.rem(me, nz)
    right = (sec, mx * nz + lax.rem(mz + 1, nz))
    left = (sec, mx * nz + lax.rem(mz + nz - 1, nz))
    sec_up, sec_down = lax.rem(sec + 1, nsec), lax.rem(sec + nsec - 1, nsec)
    columns = [lax.rem(mx + i, nx) for i in range(nx)]
    targets = [lax.rem(mx + nx - i, nx) for i in range(nx)]
    out_way = (right, left)
    back_way = (left, right)

    def remote(src, dst, send, recv, device):
        return pltpu.make_async_remote_copy(
            src_ref=src, dst_ref=dst, send_sem=send, recv_sem=recv, device_id=device, device_id_type=MESH
        )

    def sub(i):
        return pl.ds(i * SUB, SUB)

    def sub_at(index):
        return pl.ds(pl.multiple_of(index * SUB, SUB), SUB)

    peers = [right, left]
    peers += [(sec, columns[i] * nz + mz) for i in range(1, nx)]
    peers += [(s, columns[i] * nz + mz) for s in (sec_up, sec_down) for i in range(nx)]
    barrier = pltpu.get_barrier_semaphore()
    for peer in peers:
        pl.semaphore_signal(barrier, inc=1, device_id=peer, device_id_type=MESH)

    loads = [
        pltpu.make_async_copy(src, dst, load_sem.at[k])
        for k, (src, dst) in enumerate((
            (idf_hbm, ids.at[0]), (gf_hbm, gates.at[0]), (idb_hbm, ids.at[1]), (gb_hbm, gates.at[1]),
            (x_hbm, xin.at[0]), (dy_hbm, xin.at[1]),
            (up_hbm, upw.at[:, pl.ds(0, hid)]), (down_hbm, downw.at[pl.ds(0, hid)]), (saved_hbm, saved),
        ))
    ]
    for load in loads:
        load.start()

    for load in loads[:4]:
        load.wait()
    places, weights = routing(ids[0], gates[0], ids[1], gates[1], nx)
    blank = jnp.zeros_like(places[0][0])
    chosen_f = jnp.concatenate([piece for e in range(nx) for piece in (places[0][e], blank)]).astype(bf16)
    chosen_b = jnp.concatenate([piece for e in range(nx) for piece in (blank, places[1][e])]).astype(bf16)
    weight = jnp.concatenate([weights[h][e] for e in range(nx) for h in range(2)])
    gall[...] = jnp.broadcast_to(weight, gall.shape)
    for load in loads[4:6]:
        load.wait()

    for step in range(width // tile):
        cols = pl.ds(step * tile, tile)
        rows[:, cols] = (
            jnp.dot(chosen_f, xin[0, :, cols], preferred_element_type=f32)
            + jnp.dot(chosen_b, xin[1, :, cols], preferred_element_type=f32)
        ).astype(bf16)

    ag[0, 0, sub(0)] = rows[sub_at(mx)]
    gown[sub(0)] = gall[sub_at(mx)]
    pl.semaphore_wait(barrier, len(peers))

    def row_copy(i, side):
        device = (sec, targets[i] * nz + mz)
        src, dst = rows.at[sub_at(targets[i]), sides[side]], ag.at[0, 0, sub(i), sides[side]]
        return remote(src, dst, xs_send.at[i - 1, side], xs_recv.at[i - 1, side], device)

    def gate_copy(i):
        device = (sec, targets[i] * nz + mz)
        return remote(
            gall.at[sub_at(targets[i])], gown.at[sub(i)], gs_send.at[i - 1], gs_recv.at[i - 1], device
        )

    def own_copy(d, i, cols):
        src, dst = ag.at[0, 0, sub(i), cols], ag.at[1, d, sub(i), cols]
        return remote(src, dst, ag_send.at[d], ag_recv.at[1, d, i], out_way[d])

    def out_copy(s, d, i):
        src, dst = ag.at[s, d, sub(i)], ag.at[s + 1, d, sub(i)]
        return remote(src, dst, ag_send.at[s + 1], ag_recv.at[s + 1, d, i], out_way[d])

    def far_copy(d, i):
        src, dst = ag.at[half - 1, d, sub(i), sides[d]], ag.at[0, 1, sub(i), sides[d]]
        return remote(src, dst, ag_send.at[half + d], ag_recv.at[0, d, i], out_way[d])

    for d in range(2):
        own_copy(d, 0, pl.ds(0, width)).start()
    pieces = [(i, side) for group in (seq[1:3], seq[3:]) for side in range(2) for i in group]
    for i, side in pieces:
        row_copy(i, side).start()
    for i in range(1, nx):
        gate_copy(i).start()

    next_of = ((sec_up, me), (sec_down, me))
    near_copies = [
        remote(src.at[h], dst.at[h], near_send.at[h, k], near_recv.at[h, k], next_of[h])
        for h in range(2)
        for k, (src, dst) in enumerate(((xin, near), (plr, near_plr)))
    ]
    near_copies[0].start()
    near_copies[2].start()

    for i, side in pieces:
        row_copy(i, side).wait_recv()
        for d in range(2):
            own_copy(d, i, sides[side]).start()

    for load in loads[6:]:
        load.wait()

    @pl.loop(0, width // tile)
    def _(step):
        cols = pl.ds(pl.multiple_of(step * tile, tile), tile)
        upw[cols, pl.ds(hid, hid)] = downw[pl.ds(0, hid), cols].T
        downw[pl.ds(hid, hid), cols] = upw[cols, pl.ds(0, hid)].T

    @pl.loop(0, nx)
    def _(column):
        value = saved[column]
        sig = jax.nn.sigmoid(value)
        saved[column] = sig * (1.0 + value * (1.0 - sig))

    for h in range(2):
        pairs = [[places[h][e], blank] for e in range(nx)] + [[blank, places[h][e]] for e in range(nx)]
        spots = jnp.concatenate([piece for pair in pairs for piece in pair])
        plr[h] = spots.T.astype(bf16)
        near_copies[2 * h + 1].start()

    def compute(s, first, sources):
        count = len(sources)
        blocks = pl.ds(first, count)

        def add_up(step, total):
            cols = pl.ds(pl.multiple_of(step * tile, tile), tile)
            block = ag[s, blocks, :, cols].reshape(count * span, tile)
            return total + jnp.dot(block, upw[cols, :], preferred_element_type=f32)

        total = lax.fori_loop(0, width // tile, add_up, jnp.zeros((count * span, 2 * hid), f32))
        total = total.reshape(count * nx, 2, CAP, 2 * hid)
        forward = total[:, 0, :, :hid]
        forward = forward * jax.nn.sigmoid(forward)
        slope = jnp.stack([saved[columns[i], source] for source in sources for i in range(nx)])
        backward = total[:, 1, :, hid:] * slope
        none = jnp.zeros_like(forward)
        inner = jnp.stack(
            [jnp.concatenate([forward, none], axis=-1), jnp.concatenate([none, backward], axis=-1)], axis=1
        )
        inner = inner.reshape(count * span, 2 * hid).astype(bf16)

        def take_down(step, top):
            cols = pl.ds(pl.multiple_of(step * tile, tile), tile)
            result = jnp.dot(inner, downw[:, cols], preferred_element_type=f32).astype(bf16)
            part[s, blocks, :, cols] = result.reshape(count, span, tile)
            size = jnp.abs(result.astype(f32))
            for k in range(tile // 128):
                top = jnp.maximum(top, size[:, k * 128 : (k + 1) * 128])
            return top

        top = lax.fori_loop(0, width // tile, take_down, jnp.zeros((count * span, 128), f32))
        top = jnp.max(top, axis=1, keepdims=True)
        lane_group = lax.div(lax.broadcasted_iota(i32, (SUB, 128), 1), group)
        for k in range(count):
            spread = jnp.zeros((SUB, 128), f32)
            for i in range(nx):
                start = k * span + i * SUB
                spread = jnp.where(lane_group == i, top[start : start + SUB], spread)
            bound[s, first + k] = spread

    def both(s):
        return (lax.rem(mz + nz - s, nz), lax.rem(mz + s, nz))

    @pl.loop(1, half - 1)
    def _(s):
        for i in seq:
            for d in range(2):
                out_copy(s - 1, d, i).wait_recv()
                out_copy(s, d, i).start()
        compute(s, 0, both(s))

    for i in seq:
        for d in range(2):
            out_copy(half - 2, d, i).wait_recv()
            far_copy(d, i).start()
    compute(half - 1, 0, both(half - 1))

    def level_copy(k, to, d):
        return remote(level_out.at[k, d], level_in.at[to, d], lv_send.at[k, d], lv_recv.at[to, d], back_way[d])

    def bound_in(k, d):
        return TOP_CODE * jnp.exp(level_in[k, d].astype(i32).astype(f32) * (1.0 / LEVELS))

    def send_level(k, to, d, most):
        level = jnp.ceil(jnp.log(jnp.maximum(most, 1e-30) * (1.0 / TOP_CODE)) * LEVELS)
        level_out[k, d] = level.astype(i32).astype(i16)
        level_copy(k, to, d).start()

    def level_of(ref, k, d, i):
        return ref[k, d].astype(i32).astype(f32)[:, i * group : i * group + 1]

    def write(ref, i, side, value, k, d):
        codes = jnp.round(value * jnp.exp(level_of(level_out, k, d, i) * (-1.0 / LEVELS)))
        ref[sub(i), sides[side]] = codes.astype(i32).astype(i16)

    def read(ref, i, side, k, d):
        codes = ref[sub(i), sides[side]].astype(i32).astype(f32)
        return codes * jnp.exp(level_of(level_in, k, d, i) * (1.0 / LEVELS))

    def term(s, d, i, side):
        return part[s, d, sub(i), sides[side]].astype(f32)

    def back_copy(s, d, i):
        src, dst = rs.at[s, d, sub(i)], rs.at[s - 1, d, sub(i)]
        return remote(src, dst, rs_send.at[s], rs_recv.at[s - 1, d, i], back_way[d])

    def half_copy(d, i, side):
        src, dst = rs.at[half - 1, d, sub(i), sides[side]], rs.at[half - 2, d, sub(i), sides[side]]
        return remote(src, dst, rs_send.at[half - 1], rs_recv.at[half - 2, d, i], back_way[d])

    def first_copy(d, i):
        src, dst = stage.at[sub(i), sides[d]], rs.at[half - 1, d, sub(i), sides[d]]
        return remote(src, dst, rs_send.at[0], rs_recv.at[half - 1, d, i], back_way[d])

    def last_copy(d, i, side):
        src, dst = rs.at[1, d, sub(i), sides[side]], rs.at[0, d, sub(i), sides[side]]
        return remote(src, dst, rs_send.at[1], last_recv.at[d, i, side], back_way[d])

    for d in range(2):
        send_level(half, half, d, bound[half - 1, d])
    for i in back_seq:
        for d in range(2):
            write(rs.at[half - 1, d], i, 1 - d, term(half - 1, d, i, 1 - d), half, d)
            half_copy(d, i, 1 - d).start()
    for i in seq:
        for d in range(2):
            far_copy(d, i).wait_recv()
    compute(0, 1, (lax.rem(mz + half, nz),))
    for d in range(2):
        send_level(0, half - 1, d, bound[0, 1])
    for i in back_seq:
        for d in range(2):
            write(stage, i, d, term(0, 1, i, d), 0, d)
            first_copy(d, i).start()
    compute(0, 0, (mz,))
    for d in range(2):
        level_copy(0, half - 1, d).wait_recv()
        send_level(half - 1, half - 2, d, bound_in(half - 1, d) + bound[half - 1, d])
    for i in back_seq:
        for d in range(2):
            first_copy(d, i).wait_recv()
            ref = rs.at[half - 1, d]
            write(ref, i, d, read(ref, i, d, half - 1, d) + term(half - 1, d, i, d), half - 1, d)
            half_copy(d, i, d).start()

    def settle(s):
        remote(ag.at[s], ag.at[s], ag_send.at[s + 1], ag_recv.at[s, 0, 0], right).wait_send()

    for d in range(2):
        level_copy(half, half, d).wait_recv()
        level_copy(half - 1, half - 2, d).wait_recv()
        most = jnp.maximum(bound_in(half, d), bound_in(half - 2, d))
        send_level(half - 2, half - 3, d, most + bound[half - 2, d])
    for i in back_seq:
        for d in range(2):
            back_copy(half - 1, d, i).wait_recv()
            ref = rs.at[half - 2, d]
            for side in range(2):
                level = half - 2 if side == d else half
                write(ref, i, side, read(ref, i, side, level, d) + term(half - 2, d, i, side), half - 2, d)
            back_copy(half - 2, d, i).start()
    settle(half - 2)

    @pl.loop(1, half - 3)
    def _(step):
        s = half - 2 - step
        for d in range(2):
            level_copy(s + 1, s, d).wait_recv()
            send_level(s, s - 1, d, bound_in(s, d) + bound[s, d])
        for i in back_seq:
            for d in range(2):
                back_copy(s + 1, d, i).wait_recv()
                ref = rs.at[s, d]
                for side in range(2):
                    write(ref, i, side, read(ref, i, side, s, d) + term(s, d, i, side), s, d)
                back_copy(s, d, i).start()
        settle(s)

    for d in range(2):
        level_copy(2, 1, d).wait_recv()
        send_level(1, 0, d, bound_in(1, d) + bound[1, d])
    for i in back_seq:
        for d in range(2):
            back_copy(2, d, i).wait_recv()
        for side in range(2):
            for d in range(2):
                ref = rs.at[1, d]
                write(ref, i, side, read(ref, i, side, 1, d) + term(1, d, i, side), 1, d)
                last_copy(d, i, side).start()
    settle(1)

    for i in range(1, nx):
        gate_copy(i).wait_recv()

    quarter = fold // 2

    def y_copy(h, i, side):
        device = ((sec_up, sec_down)[h], columns[i] * nz + mz)
        cols = pl.ds(side * quarter, quarter)
        src, dst = ysend.at[h, sub(i), cols], yrecv.at[h, sub_at(mx), cols]
        return remote(src, dst, y_send.at[h], y_recv.at[h, mx], device)

    for i in range(1, nx):
        for side in range(2):
            row_copy(i, side).wait_send()
        gate_copy(i).wait_send()
    for d in range(2):
        remote(ag.at[0, 0], ag.at[1, d], ag_send.at[d], ag_recv.at[1, d, 0], right).wait_send()
        far = ag.at[half - 1, d, :, sides[d]]
        remote(far, far, ag_send.at[half + d], ag_recv.at[0, 1, 0], right).wait_send()
    remote(stage, rs.at[0, 0], rs_send.at[0], rs_recv.at[0, 0, 0], right).wait_send()
    for s in range(2, half):
        remote(rs.at[s], rs.at[s - 1], rs_send.at[s], rs_recv.at[0, 0, 0], right).wait_send()
    for d in range(2):
        level_copy(1, 0, d).wait()
        for k in (0, *range(2, half + 1)):
            level_copy(k, 0, d).wait_send()
    for copy in near_copies:
        copy.wait()

    for i in back_seq:
        gate = gown[sub(i), 0:1]
        for side in range(2):
            for d in range(2):
                last_copy(d, i, side).wait_recv()
            total = term(0, 0, i, side)
            for d in range(2):
                total = total + read(rs.at[0, d], i, side, 0, d)
            value = ag[0, 0, sub(i), sides[side]].astype(f32) + gate * total
            for h in range(2):
                picked = value[h * CAP : (h + 1) * CAP]
                folded = jnp.concatenate([picked[:, :quarter], picked[:, quarter:]], axis=0)
                ysend[h, sub(i), pl.ds(side * quarter, quarter)] = folded.astype(bf16)
                y_copy(h, i, side).start()

    for h in range(2):
        for e in range(nx):
            remote(ysend.at[h, sub(e)], yrecv.at[h, sub(e)], y_send.at[h], y_recv.at[h, e], next_of[h]).wait_recv()

    for d in range(2):
        remote(ysend.at[d], yrecv.at[d], y_send.at[d], y_recv.at[d, 0], right).wait_send()
    remote(rs.at[1], rs.at[0], rs_send.at[1], rs_recv.at[0, 0, 0], right).wait_send()


def place_rows(near, places, moved, outf, outb, done, out_sem):
    width = near.shape[2]
    fold = width // 2
    span = moved.shape[1]
    stores = []
    quarter = fold // 2
    for h in range(2):
        place = places[h]
        with_share = jnp.max(place.astype(f32), axis=1, keepdims=True) > 0.5
        for side in range(2):
            share = moved[h, :, side * quarter : (side + 1) * quarter]
            for k in range(2):
                cols = pl.ds((2 * side + k) * quarter, quarter)
                spots = place[:, k * span : (k + 1) * span]
                here = jnp.dot(spots, share, preferred_element_type=f32)
                done[h, :, cols] = jnp.where(with_share, here, near[h, :, cols].astype(f32)).astype(bf16)
            cols = pl.ds(side * fold, fold)
            store = pltpu.make_async_copy(done.at[h, :, cols], (outf, outb)[h].at[:, cols], out_sem.at[h, side])
            store.start()
            stores.append(store)
    for store in stores:
        store.wait()


def per_device(x_fwd, ids_fwd, gates_fwd, dy_bwd, ids_bwd, gates_bwd, saved_hidden, w_up, w_down):
    nsec = lax.axis_size("section")
    devices = lax.axis_size("expert")
    hid = w_up.shape[2]
    nz = FF // hid
    nx = devices // nz
    half = nz // 2
    tokens, width = x_fwd.shape[1:]
    span = SUB * nx
    choices = ids_fwd.shape[2]
    any_space = pl.BlockSpec(memory_space=pl.ANY)
    vmem = pl.BlockSpec(memory_space=pltpu.VMEM)
    dma = pltpu.SemaphoreType.DMA
    near, near_plr, yrecv = pl.pallas_call(
        functools.partial(kernel, nsec, nx, nz),
        out_shape=[
            pltpu.VMEM((2, tokens, width), bf16),
            pltpu.VMEM((2, tokens, 2 * span), bf16),
            pltpu.VMEM((2, span, width // 2), bf16),
        ],
        in_specs=[any_space] * 9,
        out_specs=[vmem] * 3,
        scratch_shapes=[
            pltpu.VMEM((half + 1, 2, SUB, 128), i16),
            pltpu.VMEM((half + 1, 2, SUB, 128), i16),
            pltpu.VMEM((half, 2, SUB, 128), f32),
            pltpu.VMEM((2, tokens, width), bf16),
            pltpu.VMEM((2, choices, tokens), i32),
            pltpu.VMEM((2, choices, tokens), f32),
            pltpu.VMEM((span, width), bf16),
            pltpu.VMEM((span, 128), f32),
            pltpu.VMEM((span, 128), f32),
            pltpu.VMEM((width, 2 * hid), bf16),
            pltpu.VMEM((2 * hid, width), bf16),
            pltpu.VMEM((nx, nz, CAP, hid), f32),
            pltpu.VMEM((half, 2, span, width), bf16),
            pltpu.VMEM((half, 2, span, width), i16),
            pltpu.VMEM((span, width), i16),
            pltpu.VMEM((half, 2, span, width), bf16),
            pltpu.VMEM((2, tokens, 2 * span), bf16),
            pltpu.VMEM((2, span, width // 2), bf16),
            dma((9,)),
            dma((nx - 1, 2)), dma((nx - 1, 2)), dma((nx - 1,)), dma((nx - 1,)),
            dma((half + 2,)), dma((half, 2, nx)),
            dma((half,)), dma((half, 2, nx)),
            dma((2, 2)), dma((2, 2)), dma((2,)), dma((2, nx)), dma((2, nx, 2)), dma((half + 1, 2)), dma((half + 1, 2)),
        ],
        compiler_params=pltpu.CompilerParams(
            collective_id=0, has_side_effects=True, vmem_limit_bytes=56 * 1024 * 1024
        ),
    )(
        x_fwd[0], dy_bwd[0], ids_fwd[0].T, gates_fwd[0].T, ids_bwd[0].T, gates_bwd[0].T,
        saved_hidden[0].reshape(nx, nz, CAP, hid), w_up[0], w_down[0],
    )
    outs = pl.pallas_call(
        place_rows,
        out_shape=[jax.ShapeDtypeStruct((tokens, width), bf16)] * 2,
        in_specs=[vmem] * 3,
        out_specs=[any_space] * 2,
        scratch_shapes=[pltpu.VMEM((2, tokens, width), bf16), dma((2, 2))],
        compiler_params=pltpu.CompilerParams(vmem_limit_bytes=32 * 1024 * 1024),
    )(*(pltpu.with_memory_space_constraint(v, pltpu.VMEM) for v in (near, near_plr, yrecv)))
    return (outs[0][None], outs[1][None])


def solution(mesh):
    in_specs = (
        P("section", "expert", None),
        P("section", "expert", None),
        P("section", "expert", None),
        P("section", "expert", None),
        P("section", "expert", None),
        P("section", "expert", None),
        P("section", None, "expert"),
        P("section", None, "expert"),
        P("section", "expert", None),
    )
    out_specs = (P("section", "expert", None), P("section", "expert", None))
    return jax.shard_map(
        per_device, mesh=mesh, in_specs=in_specs, out_specs=out_specs, check_vma=False
    )
```

```python
import functools
import math

import jax
import jax.numpy as jnp
from jax import lax
from jax.experimental import pallas as pl
from jax.experimental.pallas import tpu as pltpu
from jax.sharding import PartitionSpec as P

MESH = pl.DeviceIdType.MESH
CAP = 8
SUB = 2 * CAP
FF = 2048
TOP_CODE = 32000.0
LEVELS = 256 / math.log(2)
f32 = jnp.float32
bf16 = jnp.bfloat16
i32 = jnp.int32
i16 = jnp.int16


def tile_of(width):
    return 512 if width % 512 == 0 else 128


def routing(ids_f, gates_f, ids_b, gates_b, window):
    rows = ids_f.shape[1]
    routed, gates = [], []
    for ids, values in ((ids_f, gates_f), (ids_b, gates_b)):
        for e in range(window):
            match = ids == e
            routed.append(jnp.max(jnp.where(match, 1.0, 0.0), axis=0, keepdims=True))
            gates.append(jnp.sum(jnp.where(match, values, 0.0), axis=0, keepdims=True))
    earlier = lax.broadcasted_iota(i32, (rows, rows), 0) < lax.broadcasted_iota(
        i32, (rows, rows), 1
    )
    position = jnp.dot(
        jnp.concatenate(routed, axis=0).astype(bf16),
        jnp.where(earlier, 1.0, 0.0).astype(bf16),
        preferred_element_type=f32,
    )
    slot = lax.broadcasted_iota(i32, (CAP, rows), 0).astype(f32)
    places, weights = [], []
    for k in range(2 * window):
        place = jnp.where((position[k : k + 1] == slot) & (routed[k] > 0.5), 1.0, 0.0)
        places.append(place)
        weights.append(jnp.sum(place * gates[k], axis=1, keepdims=True))
    return (places[:window], places[window:]), (weights[:window], weights[window:])


def kernel(
    nsec, nx, nz,
    x_hbm, dy_hbm, idf_hbm, gf_hbm, idb_hbm, gb_hbm, saved_hbm, up_hbm, down_hbm,
    near, near_plr, yrecv,
    level_in, level_out, bound,
    xin, ids, gates, rows, gall, gown, upw, downw, saved, ag, rs, stage, part, plr, ysend,
    load_sem, xs_send, xs_recv, gs_send, gs_recv, ag_send, ag_recv, rs_send, rs_recv,
    near_send, near_recv, y_send, y_recv, last_recv, lv_send, lv_recv,
):
    half = nz // 2
    width = xin.shape[2]
    span = SUB * nx
    fold = width // 2
    hid = upw.shape[1] // 2
    tile = tile_of(width)
    seq = (0, 1, 3, 2) if nx == 4 else tuple(range(nx))
    back_seq = seq[::-1]
    twos = range(nx // 2)
    sides = (pl.ds(0, fold), pl.ds(fold, fold))
    quarter = fold // 2
    quarters = [pl.ds(k * quarter, quarter) for k in range(4)]
    group = 128 // nx

    sec = lax.axis_index("section")
    me = lax.axis_index("expert")
    mx, mz = lax.div(me, nz), lax.rem(me, nz)
    right = (sec, mx * nz + lax.rem(mz + 1, nz))
    left = (sec, mx * nz + lax.rem(mz + nz - 1, nz))
    sec_up, sec_down = lax.rem(sec + 1, nsec), lax.rem(sec + nsec - 1, nsec)
    columns = [lax.rem(mx + i, nx) for i in range(nx)]
    targets = [lax.rem(mx + nx - i, nx) for i in range(nx)]
    out_way = (right, left)
    back_way = (left, right)

    def remote(src, dst, send, recv, device):
        return pltpu.make_async_remote_copy(
            src_ref=src, dst_ref=dst, send_sem=send, recv_sem=recv, device_id=device, device_id_type=MESH
        )

    def sub(i):
        return pl.ds(i * SUB, SUB)

    def pair(p):
        return pl.ds(p * 2 * SUB, 2 * SUB)

    def sub_at(index):
        return pl.ds(pl.multiple_of(index * SUB, SUB), SUB)

    peers = [right, left]
    peers += [(sec, columns[i] * nz + mz) for i in range(1, nx)]
    peers += [(s, columns[i] * nz + mz) for s in (sec_up, sec_down) for i in range(nx)]
    barrier = pltpu.get_barrier_semaphore()
    for peer in peers:
        pl.semaphore_signal(barrier, inc=1, device_id=peer, device_id_type=MESH)

    loads = [
        pltpu.make_async_copy(src, dst, load_sem.at[k])
        for k, (src, dst) in enumerate((
            (idf_hbm, ids.at[0]), (gf_hbm, gates.at[0]), (idb_hbm, ids.at[1]), (gb_hbm, gates.at[1]),
            (x_hbm, xin.at[0]), (dy_hbm, xin.at[1]),
            (up_hbm, upw.at[:, pl.ds(0, hid)]), (down_hbm, downw.at[pl.ds(0, hid)]), (saved_hbm, saved),
        ))
    ]
    for load in loads:
        load.start()

    for load in loads[:4]:
        load.wait()
    places, weights = routing(ids[0], gates[0], ids[1], gates[1], nx)
    blank = jnp.zeros_like(places[0][0])
    chosen_f = jnp.concatenate([piece for e in range(nx) for piece in (places[0][e], blank)]).astype(bf16)
    chosen_b = jnp.concatenate([piece for e in range(nx) for piece in (blank, places[1][e])]).astype(bf16)
    weight = jnp.concatenate([weights[h][e] for e in range(nx) for h in range(2)])
    gall[...] = jnp.broadcast_to(weight, gall.shape)
    for load in loads[4:6]:
        load.wait()

    for step in range(width // tile):
        cols = pl.ds(step * tile, tile)
        rows[:, cols] = (
            jnp.dot(chosen_f, xin[0, :, cols], preferred_element_type=f32)
            + jnp.dot(chosen_b, xin[1, :, cols], preferred_element_type=f32)
        ).astype(bf16)

    ag[0, 0, sub(0)] = rows[sub_at(mx)]
    gown[sub(0)] = gall[sub_at(mx)]
    pl.semaphore_wait(barrier, len(peers))

    def row_copy(i, side):
        device = (sec, targets[i] * nz + mz)
        src, dst = rows.at[sub_at(targets[i]), quarters[side]], ag.at[0, 0, sub(i), quarters[side]]
        return remote(src, dst, xs_send.at[i - 1, side], xs_recv.at[i - 1, side], device)

    def gate_copy(i):
        device = (sec, targets[i] * nz + mz)
        return remote(
            gall.at[sub_at(targets[i])], gown.at[sub(i)], gs_send.at[i - 1], gs_recv.at[i - 1], device
        )

    def own_copy(d, i, cols):
        src, dst = ag.at[0, 0, sub(i), cols], ag.at[1, d, sub(i), cols]
        return remote(src, dst, ag_send.at[d], ag_recv.at[1, d, i // 2], out_way[d])

    def out_copy(s, d, p):
        src, dst = ag.at[s, d, pair(p)], ag.at[s + 1, d, pair(p)]
        return remote(src, dst, ag_send.at[s + 1], ag_recv.at[s + 1, d, p], out_way[d])

    def far_copy(d, p):
        src, dst = ag.at[half - 1, d, pair(p), sides[d]], ag.at[0, 1, pair(p), sides[d]]
        return remote(src, dst, ag_send.at[half + d], ag_recv.at[0, d, p], out_way[d])

    for d in range(2):
        own_copy(d, 0, pl.ds(0, width)).start()
    pieces = [(i, side) for part_of in (seq[1:3], seq[3:]) for side in range(4) for i in part_of]
    for i, side in pieces:
        row_copy(i, side).start()
    for i in range(1, nx):
        gate_copy(i).start()

    next_of = ((sec_up, me), (sec_down, me))
    near_copies = [
        remote(src.at[h], dst.at[h], near_send.at[h, k], near_recv.at[h, k], next_of[h])
        for h in range(2)
        for k, (src, dst) in enumerate(((xin, near), (plr, near_plr)))
    ]
    for i, side in pieces:
        row_copy(i, side).wait_recv()
        for d in range(2):
            own_copy(d, i, quarters[side]).start()

    for load in loads[6:]:
        load.wait()

    @pl.loop(0, width // tile)
    def _(step):
        cols = pl.ds(pl.multiple_of(step * tile, tile), tile)
        upw[cols, pl.ds(hid, hid)] = downw[pl.ds(0, hid), cols].T
        downw[pl.ds(hid, hid), cols] = upw[cols, pl.ds(0, hid)].T

    @pl.loop(0, nx)
    def _(column):
        value = saved[column]
        sig = jax.nn.sigmoid(value)
        saved[column] = sig * (1.0 + value * (1.0 - sig))

    near_copies[0].start()
    near_copies[2].start()
    for h in range(2):
        pairs = [[places[h][e], blank] for e in range(nx)] + [[blank, places[h][e]] for e in range(nx)]
        spots = jnp.concatenate([piece for pair in pairs for piece in pair])
        plr[h] = spots.T.astype(bf16)
        near_copies[2 * h + 1].start()

    def compute(s, first, sources):
        count = len(sources)
        blocks = pl.ds(first, count)

        def add_up(step, total):
            cols = pl.ds(pl.multiple_of(step * tile, tile), tile)
            block = ag[s, blocks, :, cols].reshape(count * span, tile)
            return total + jnp.dot(block, upw[cols, :], preferred_element_type=f32)

        total = lax.fori_loop(0, width // tile, add_up, jnp.zeros((count * span, 2 * hid), f32))
        total = total.reshape(count * nx, 2, CAP, 2 * hid)
        forward = total[:, 0, :, :hid]
        forward = forward * jax.nn.sigmoid(forward)
        slope = jnp.stack([saved[columns[i], source] for source in sources for i in range(nx)])
        backward = total[:, 1, :, hid:] * slope
        none = jnp.zeros_like(forward)
        inner = jnp.stack(
            [jnp.concatenate([forward, none], axis=-1), jnp.concatenate([none, backward], axis=-1)], axis=1
        )
        inner = inner.reshape(count * span, 2 * hid).astype(bf16)

        def take_down(step, top):
            cols = pl.ds(pl.multiple_of(step * tile, tile), tile)
            result = jnp.dot(inner, downw[:, cols], preferred_element_type=f32).astype(bf16)
            part[s, blocks, :, cols] = result.reshape(count, span, tile)
            size = jnp.abs(result.astype(f32))
            for k in range(tile // 128):
                top = jnp.maximum(top, size[:, k * 128 : (k + 1) * 128])
            return top

        top = lax.fori_loop(0, width // tile, take_down, jnp.zeros((count * span, 128), f32))
        top = jnp.max(top, axis=1, keepdims=True)
        lane_group = lax.div(lax.broadcasted_iota(i32, (SUB, 128), 1), group)
        for k in range(count):
            spread = jnp.zeros((SUB, 128), f32)
            for i in range(nx):
                start = k * span + i * SUB
                spread = jnp.where(lane_group == i, top[start : start + SUB], spread)
            bound[s, first + k] = spread

    def both(s):
        return (lax.rem(mz + nz - s, nz), lax.rem(mz + s, nz))

    @pl.loop(1, half - 1)
    def _(s):
        for p in twos:
            for d in range(2):
                out_copy(s - 1, d, p).wait_recv()
                out_copy(s, d, p).start()
        compute(s, 0, both(s))

    for p in twos:
        for d in range(2):
            out_copy(half - 2, d, p).wait_recv()
            far_copy(d, p).start()
    compute(half - 1, 0, both(half - 1))

    def level_copy(k, to, d):
        return remote(level_out.at[k, d], level_in.at[to, d], lv_send.at[k, d], lv_recv.at[to, d], back_way[d])

    def bound_in(k, d):
        return TOP_CODE * jnp.exp(level_in[k, d].astype(i32).astype(f32) * (1.0 / LEVELS))

    def send_level(k, to, d, most):
        level = jnp.ceil(jnp.log(jnp.maximum(most, 1e-30) * (1.0 / TOP_CODE)) * LEVELS)
        level_out[k, d] = level.astype(i32).astype(i16)
        level_copy(k, to, d).start()

    def level_of(ref, k, d, i):
        return ref[k, d].astype(i32).astype(f32)[:, i * group : i * group + 1]

    def write(ref, i, side, value, k, d):
        codes = jnp.round(value * jnp.exp(level_of(level_out, k, d, i) * (-1.0 / LEVELS)))
        ref[sub(i), sides[side]] = codes.astype(i32).astype(i16)

    def read(ref, i, side, k, d):
        codes = ref[sub(i), sides[side]].astype(i32).astype(f32)
        return codes * jnp.exp(level_of(level_in, k, d, i) * (1.0 / LEVELS))

    def term(s, d, i, side):
        return part[s, d, sub(i), sides[side]].astype(f32)

    def back_copy(s, d, p):
        src, dst = rs.at[s, d, pair(p)], rs.at[s - 1, d, pair(p)]
        return remote(src, dst, rs_send.at[s], rs_recv.at[s - 1, d, p], back_way[d])

    def half_copy(d, i, side):
        src, dst = rs.at[half - 1, d, sub(i), sides[side]], rs.at[half - 2, d, sub(i), sides[side]]
        return remote(src, dst, rs_send.at[half - 1], rs_recv.at[half - 2, d, i // 2], back_way[d])

    def first_copy(d, i):
        src, dst = stage.at[sub(i), sides[d]], rs.at[half - 1, d, sub(i), sides[d]]
        return remote(src, dst, rs_send.at[0], rs_recv.at[half - 1, d, i], back_way[d])

    def last_copy(d, i, side):
        src, dst = rs.at[1, d, sub(i), sides[side]], rs.at[0, d, sub(i), sides[side]]
        return remote(src, dst, rs_send.at[1], last_recv.at[d, i, side], back_way[d])

    for d in range(2):
        send_level(half, half, d, bound[half - 1, d])
    for i in back_seq:
        for d in range(2):
            write(rs.at[half - 1, d], i, 1 - d, term(half - 1, d, i, 1 - d), half, d)
            half_copy(d, i, 1 - d).start()
    for p in twos:
        for d in range(2):
            far_copy(d, p).wait_recv()
    compute(0, 1, (lax.rem(mz + half, nz),))
    for d in range(2):
        send_level(0, half - 1, d, bound[0, 1])
    for i in back_seq:
        for d in range(2):
            write(stage, i, d, term(0, 1, i, d), 0, d)
            first_copy(d, i).start()
    compute(0, 0, (mz,))
    for d in range(2):
        level_copy(0, half - 1, d).wait_recv()
        send_level(half - 1, half - 2, d, bound_in(half - 1, d) + bound[half - 1, d])
    for i in back_seq:
        for d in range(2):
            first_copy(d, i).wait_recv()
            ref = rs.at[half - 1, d]
            write(ref, i, d, read(ref, i, d, half - 1, d) + term(half - 1, d, i, d), half - 1, d)
            half_copy(d, i, d).start()

    def settle(s):
        remote(ag.at[s], ag.at[s], ag_send.at[s + 1], ag_recv.at[s, 0, 0], right).wait_send()

    for d in range(2):
        level_copy(half, half, d).wait_recv()
        level_copy(half - 1, half - 2, d).wait_recv()
        most = jnp.maximum(bound_in(half, d), bound_in(half - 2, d))
        send_level(half - 2, half - 3, d, most + bound[half - 2, d])
    for p in twos[::-1]:
        for d in range(2):
            back_copy(half - 1, d, p).wait_recv()
            ref = rs.at[half - 2, d]
            for i in (2 * p, 2 * p + 1):
                for side in range(2):
                    level = half - 2 if side == d else half
                    write(ref, i, side, read(ref, i, side, level, d) + term(half - 2, d, i, side), half - 2, d)
            back_copy(half - 2, d, p).start()
    settle(half - 2)

    @pl.loop(1, half - 3)
    def _(step):
        s = half - 2 - step
        for d in range(2):
            level_copy(s + 1, s, d).wait_recv()
            send_level(s, s - 1, d, bound_in(s, d) + bound[s, d])
        for p in twos[::-1]:
            for d in range(2):
                back_copy(s + 1, d, p).wait_recv()
                ref = rs.at[s, d]
                for i in (2 * p, 2 * p + 1):
                    for side in range(2):
                        write(ref, i, side, read(ref, i, side, s, d) + term(s, d, i, side), s, d)
                back_copy(s, d, p).start()
        settle(s)

    for d in range(2):
        level_copy(2, 1, d).wait_recv()
        send_level(1, 0, d, bound_in(1, d) + bound[1, d])
    for k, i in enumerate(back_seq):
        for d in range(2):
            if k % 2 == 0:
                back_copy(2, d, i // 2).wait_recv()
        for side in range(2):
            for d in range(2):
                ref = rs.at[1, d]
                write(ref, i, side, read(ref, i, side, 1, d) + term(1, d, i, side), 1, d)
                last_copy(d, i, side).start()
    settle(1)

    for i in range(1, nx):
        gate_copy(i).wait_recv()

    def y_copy(h, i, side):
        device = ((sec_up, sec_down)[h], columns[i] * nz + mz)
        cols = pl.ds(side * quarter, quarter)
        src, dst = ysend.at[h, sub(i), cols], yrecv.at[h, sub_at(mx), cols]
        return remote(src, dst, y_send.at[h], y_recv.at[h, mx], device)

    for i in range(1, nx):
        for side in range(4):
            row_copy(i, side).wait_send()
        gate_copy(i).wait_send()
    for d in range(2):
        remote(ag.at[0, 0], ag.at[1, d], ag_send.at[d], ag_recv.at[1, d, 0], right).wait_send()
        far = ag.at[half - 1, d, :, sides[d]]
        remote(far, far, ag_send.at[half + d], ag_recv.at[0, 1, 0], right).wait_send()
    remote(stage, rs.at[0, 0], rs_send.at[0], rs_recv.at[0, 0, 0], right).wait_send()
    for s in range(2, half):
        remote(rs.at[s], rs.at[s - 1], rs_send.at[s], rs_recv.at[0, 0, 0], right).wait_send()
    for d in range(2):
        level_copy(1, 0, d).wait()
        for k in (0, *range(2, half + 1)):
            level_copy(k, 0, d).wait_send()
    for copy in near_copies:
        copy.wait()

    for i in back_seq:
        gate = gown[sub(i), 0:1]
        for side in range(2):
            for d in range(2):
                last_copy(d, i, side).wait_recv()
            total = term(0, 0, i, side)
            for d in range(2):
                total = total + read(rs.at[0, d], i, side, 0, d)
            value = ag[0, 0, sub(i), sides[side]].astype(f32) + gate * total
            for h in range(2):
                picked = value[h * CAP : (h + 1) * CAP]
                folded = jnp.concatenate([picked[:, :quarter], picked[:, quarter:]], axis=0)
                ysend[h, sub(i), pl.ds(side * quarter, quarter)] = folded.astype(bf16)
                y_copy(h, i, side).start()

    for h in range(2):
        for e in range(nx):
            remote(ysend.at[h, sub(e)], yrecv.at[h, sub(e)], y_send.at[h], y_recv.at[h, e], next_of[h]).wait_recv()

    for d in range(2):
        remote(ysend.at[d], yrecv.at[d], y_send.at[d], y_recv.at[d, 0], right).wait_send()
    remote(rs.at[1], rs.at[0], rs_send.at[1], rs_recv.at[0, 0, 0], right).wait_send()


def place_rows(near, places, moved, outf, outb, done, out_sem):
    width = near.shape[2]
    fold = width // 2
    span = moved.shape[1]
    stores = []
    quarter = fold // 2
    for h in range(2):
        place = places[h]
        with_share = jnp.max(place.astype(f32), axis=1, keepdims=True) > 0.5
        for side in range(2):
            share = moved[h, :, side * quarter : (side + 1) * quarter]
            for k in range(2):
                cols = pl.ds((2 * side + k) * quarter, quarter)
                spots = place[:, k * span : (k + 1) * span]
                here = jnp.dot(spots, share, preferred_element_type=f32)
                done[h, :, cols] = jnp.where(with_share, here, near[h, :, cols].astype(f32)).astype(bf16)
            cols = pl.ds(side * fold, fold)
            store = pltpu.make_async_copy(done.at[h, :, cols], (outf, outb)[h].at[:, cols], out_sem.at[h, side])
            store.start()
            stores.append(store)
    for store in stores:
        store.wait()


def per_device(x_fwd, ids_fwd, gates_fwd, dy_bwd, ids_bwd, gates_bwd, saved_hidden, w_up, w_down):
    nsec = lax.axis_size("section")
    devices = lax.axis_size("expert")
    hid = w_up.shape[2]
    nz = FF // hid
    nx = devices // nz
    half = nz // 2
    tokens, width = x_fwd.shape[1:]
    span = SUB * nx
    choices = ids_fwd.shape[2]
    any_space = pl.BlockSpec(memory_space=pl.ANY)
    vmem = pl.BlockSpec(memory_space=pltpu.VMEM)
    dma = pltpu.SemaphoreType.DMA
    near, near_plr, yrecv = pl.pallas_call(
        functools.partial(kernel, nsec, nx, nz),
        out_shape=[
            pltpu.VMEM((2, tokens, width), bf16),
            pltpu.VMEM((2, tokens, 2 * span), bf16),
            pltpu.VMEM((2, span, width // 2), bf16),
        ],
        in_specs=[any_space] * 9,
        out_specs=[vmem] * 3,
        scratch_shapes=[
            pltpu.VMEM((half + 1, 2, SUB, 128), i16),
            pltpu.VMEM((half + 1, 2, SUB, 128), i16),
            pltpu.VMEM((half, 2, SUB, 128), f32),
            pltpu.VMEM((2, tokens, width), bf16),
            pltpu.VMEM((2, choices, tokens), i32),
            pltpu.VMEM((2, choices, tokens), f32),
            pltpu.VMEM((span, width), bf16),
            pltpu.VMEM((span, 128), f32),
            pltpu.VMEM((span, 128), f32),
            pltpu.VMEM((width, 2 * hid), bf16),
            pltpu.VMEM((2 * hid, width), bf16),
            pltpu.VMEM((nx, nz, CAP, hid), f32),
            pltpu.VMEM((half, 2, span, width), bf16),
            pltpu.VMEM((half, 2, span, width), i16),
            pltpu.VMEM((span, width), i16),
            pltpu.VMEM((half, 2, span, width), bf16),
            pltpu.VMEM((2, tokens, 2 * span), bf16),
            pltpu.VMEM((2, span, width // 2), bf16),
            dma((9,)),
            dma((nx - 1, 4)), dma((nx - 1, 4)), dma((nx - 1,)), dma((nx - 1,)),
            dma((half + 2,)), dma((half, 2, nx)),
            dma((half,)), dma((half, 2, nx)),
            dma((2, 2)), dma((2, 2)), dma((2,)), dma((2, nx)), dma((2, nx, 2)), dma((half + 1, 2)), dma((half + 1, 2)),
        ],
        compiler_params=pltpu.CompilerParams(
            collective_id=0, has_side_effects=True, vmem_limit_bytes=56 * 1024 * 1024
        ),
    )(
        x_fwd[0], dy_bwd[0], ids_fwd[0].T, gates_fwd[0].T, ids_bwd[0].T, gates_bwd[0].T,
        saved_hidden[0].reshape(nx, nz, CAP, hid), w_up[0], w_down[0],
    )
    outs = pl.pallas_call(
        place_rows,
        out_shape=[jax.ShapeDtypeStruct((tokens, width), bf16)] * 2,
        in_specs=[vmem] * 3,
        out_specs=[any_space] * 2,
        scratch_shapes=[pltpu.VMEM((2, tokens, width), bf16), dma((2, 2))],
        compiler_params=pltpu.CompilerParams(vmem_limit_bytes=32 * 1024 * 1024),
    )(*(pltpu.with_memory_space_constraint(v, pltpu.VMEM) for v in (near, near_plr, yrecv)))
    return (outs[0][None], outs[1][None])


def solution(mesh):
    in_specs = (
        P("section", "expert", None),
        P("section", "expert", None),
        P("section", "expert", None),
        P("section", "expert", None),
        P("section", "expert", None),
        P("section", "expert", None),
        P("section", None, "expert"),
        P("section", None, "expert"),
        P("section", "expert", None),
    )
    out_specs = (P("section", "expert", None), P("section", "expert", None))
    return jax.shard_map(
        per_device, mesh=mesh, in_specs=in_specs, out_specs=out_specs, check_vma=False
    )
```

```python
import functools
import math

import jax
import jax.numpy as jnp
from jax import lax
from jax.experimental import pallas as pl
from jax.experimental.pallas import tpu as pltpu
from jax.sharding import PartitionSpec as P

MESH = pl.DeviceIdType.MESH
CAP = 8
SUB = 2 * CAP
FF = 2048
TOP_CODE = 32000.0
LEVELS = 256 / math.log(2)
f32 = jnp.float32
bf16 = jnp.bfloat16
i32 = jnp.int32
i16 = jnp.int16


def tile_of(width):
    return 512 if width % 512 == 0 else 128


def routing(ids_f, gates_f, ids_b, gates_b, window):
    rows = ids_f.shape[1]
    routed, gates = [], []
    for ids, values in ((ids_f, gates_f), (ids_b, gates_b)):
        for e in range(window):
            match = ids == e
            routed.append(jnp.max(jnp.where(match, 1.0, 0.0), axis=0, keepdims=True))
            gates.append(jnp.sum(jnp.where(match, values, 0.0), axis=0, keepdims=True))
    earlier = lax.broadcasted_iota(i32, (rows, rows), 0) < lax.broadcasted_iota(
        i32, (rows, rows), 1
    )
    position = jnp.dot(
        jnp.concatenate(routed, axis=0).astype(bf16),
        jnp.where(earlier, 1.0, 0.0).astype(bf16),
        preferred_element_type=f32,
    )
    slot = lax.broadcasted_iota(i32, (CAP, rows), 0).astype(f32)
    places, weights = [], []
    for k in range(2 * window):
        place = jnp.where((position[k : k + 1] == slot) & (routed[k] > 0.5), 1.0, 0.0)
        places.append(place)
        weights.append(jnp.sum(place * gates[k], axis=1, keepdims=True))
    return (places[:window], places[window:]), (weights[:window], weights[window:])


def kernel(
    nsec, nx, nz,
    x_hbm, dy_hbm, idf_hbm, gf_hbm, idb_hbm, gb_hbm, saved_hbm, up_hbm, down_hbm,
    near, near_plr, yrecv,
    level_in, level_out, bound,
    xin, ids, gates, rows, gall, gown, upw, downw, saved, ag, rs, stage, part, plr, ysend,
    load_sem, xs_send, xs_recv, gs_send, gs_recv, ag_send, ag_recv, rs_send, rs_recv,
    near_send, near_recv, y_send, y_recv, last_recv, lv_send, lv_recv,
):
    half = nz // 2
    width = xin.shape[2]
    span = SUB * nx
    fold = width // 2
    hid = upw.shape[1] // 2
    tile = tile_of(width)
    seq = (0, 1, 3, 2) if nx == 4 else tuple(range(nx))
    back_seq = seq[::-1]
    sides = (pl.ds(0, fold), pl.ds(fold, fold))
    quarter = fold // 2
    quarters = [pl.ds(k * quarter, quarter) for k in range(4)]
    group = 128 // nx

    sec = lax.axis_index("section")
    me = lax.axis_index("expert")
    mx, mz = lax.div(me, nz), lax.rem(me, nz)
    right = (sec, mx * nz + lax.rem(mz + 1, nz))
    left = (sec, mx * nz + lax.rem(mz + nz - 1, nz))
    sec_up, sec_down = lax.rem(sec + 1, nsec), lax.rem(sec + nsec - 1, nsec)
    columns = [lax.rem(mx + i, nx) for i in range(nx)]
    targets = [lax.rem(mx + nx - i, nx) for i in range(nx)]
    out_way = (right, left)
    back_way = (left, right)

    def remote(src, dst, send, recv, device):
        return pltpu.make_async_remote_copy(
            src_ref=src, dst_ref=dst, send_sem=send, recv_sem=recv, device_id=device, device_id_type=MESH
        )

    def sub(i):
        return pl.ds(i * SUB, SUB)

    def sub_at(index):
        return pl.ds(pl.multiple_of(index * SUB, SUB), SUB)

    peers = [right, left]
    peers += [(sec, columns[i] * nz + mz) for i in range(1, nx)]
    peers += [(s, columns[i] * nz + mz) for s in (sec_up, sec_down) for i in range(nx)]
    barrier = pltpu.get_barrier_semaphore()
    for peer in peers:
        pl.semaphore_signal(barrier, inc=1, device_id=peer, device_id_type=MESH)

    loads = [
        pltpu.make_async_copy(src, dst, load_sem.at[k])
        for k, (src, dst) in enumerate((
            (idf_hbm, ids.at[0]), (gf_hbm, gates.at[0]), (idb_hbm, ids.at[1]), (gb_hbm, gates.at[1]),
            (x_hbm, xin.at[0]), (dy_hbm, xin.at[1]),
            (up_hbm, upw.at[:, pl.ds(0, hid)]), (down_hbm, downw.at[pl.ds(0, hid)]), (saved_hbm, saved),
        ))
    ]
    for load in loads:
        load.start()

    for load in loads[:4]:
        load.wait()
    places, weights = routing(ids[0], gates[0], ids[1], gates[1], nx)
    blank = jnp.zeros_like(places[0][0])
    chosen_f = jnp.concatenate([piece for e in range(nx) for piece in (places[0][e], blank)]).astype(bf16)
    chosen_b = jnp.concatenate([piece for e in range(nx) for piece in (blank, places[1][e])]).astype(bf16)
    weight = jnp.concatenate([weights[h][e] for e in range(nx) for h in range(2)])
    gall[...] = jnp.broadcast_to(weight, gall.shape)
    for load in loads[4:6]:
        load.wait()

    for step in range(width // tile):
        cols = pl.ds(step * tile, tile)
        rows[:, cols] = (
            jnp.dot(chosen_f, xin[0, :, cols], preferred_element_type=f32)
            + jnp.dot(chosen_b, xin[1, :, cols], preferred_element_type=f32)
        ).astype(bf16)

    ag[0, 0, sub(0)] = rows[sub_at(mx)]
    gown[sub(0)] = gall[sub_at(mx)]
    pl.semaphore_wait(barrier, len(peers))

    def row_copy(i, side):
        device = (sec, targets[i] * nz + mz)
        src, dst = rows.at[sub_at(targets[i]), quarters[side]], ag.at[0, 0, sub(i), quarters[side]]
        return remote(src, dst, xs_send.at[i - 1, side], xs_recv.at[i - 1, side], device)

    def gate_copy(i):
        device = (sec, targets[i] * nz + mz)
        return remote(
            gall.at[sub_at(targets[i])], gown.at[sub(i)], gs_send.at[i - 1], gs_recv.at[i - 1], device
        )

    def own_copy(d, i, cols):
        src, dst = ag.at[0, 0, sub(i), cols], ag.at[1, d, sub(i), cols]
        return remote(src, dst, ag_send.at[d], ag_recv.at[1, d, i], out_way[d])

    def out_copy(s, d, i):
        src, dst = ag.at[s, d, sub(i)], ag.at[s + 1, d, sub(i)]
        return remote(src, dst, ag_send.at[s + 1], ag_recv.at[s + 1, d, i], out_way[d])

    def far_copy(d, i):
        src, dst = ag.at[half - 1, d, sub(i), sides[d]], ag.at[0, 1, sub(i), sides[d]]
        return remote(src, dst, ag_send.at[half + d], ag_recv.at[0, d, i], out_way[d])

    for d in range(2):
        own_copy(d, 0, pl.ds(0, width)).start()
    pieces = [(i, side) for part_of in (seq[1:3], seq[3:]) for side in range(4) for i in part_of]
    for i, side in pieces:
        row_copy(i, side).start()
    for i in range(1, nx):
        gate_copy(i).start()

    next_of = ((sec_up, me), (sec_down, me))
    near_copies = [
        remote(src.at[h], dst.at[h], near_send.at[h, k], near_recv.at[h, k], next_of[h])
        for h in range(2)
        for k, (src, dst) in enumerate(((xin, near), (plr, near_plr)))
    ]
    for i, side in pieces:
        row_copy(i, side).wait_recv()
        for d in range(2):
            own_copy(d, i, quarters[side]).start()

    for load in loads[6:]:
        load.wait()

    @pl.loop(0, width // tile)
    def _(step):
        cols = pl.ds(pl.multiple_of(step * tile, tile), tile)
        upw[cols, pl.ds(hid, hid)] = downw[pl.ds(0, hid), cols].T
        downw[pl.ds(hid, hid), cols] = upw[cols, pl.ds(0, hid)].T

    @pl.loop(0, nx)
    def _(column):
        value = saved[column]
        sig = jax.nn.sigmoid(value)
        saved[column] = sig * (1.0 + value * (1.0 - sig))

    near_copies[0].start()
    near_copies[2].start()
    for h in range(2):
        pairs = [[places[h][e], blank] for e in range(nx)] + [[blank, places[h][e]] for e in range(nx)]
        spots = jnp.concatenate([piece for pair in pairs for piece in pair])
        plr[h] = spots.T.astype(bf16)
        near_copies[2 * h + 1].start()

    def compute(s, first, sources):
        count = len(sources)
        blocks = pl.ds(first, count)

        def add_up(step, total):
            cols = pl.ds(pl.multiple_of(step * tile, tile), tile)
            block = ag[s, blocks, :, cols].reshape(count * span, tile)
            return total + jnp.dot(block, upw[cols, :], preferred_element_type=f32)

        total = lax.fori_loop(0, width // tile, add_up, jnp.zeros((count * span, 2 * hid), f32))
        total = total.reshape(count * nx, 2, CAP, 2 * hid)
        forward = total[:, 0, :, :hid]
        forward = forward * jax.nn.sigmoid(forward)
        slope = jnp.stack([saved[columns[i], source] for source in sources for i in range(nx)])
        backward = total[:, 1, :, hid:] * slope
        none = jnp.zeros_like(forward)
        inner = jnp.stack(
            [jnp.concatenate([forward, none], axis=-1), jnp.concatenate([none, backward], axis=-1)], axis=1
        )
        inner = inner.reshape(count * span, 2 * hid).astype(bf16)

        def take_down(step, top):
            cols = pl.ds(pl.multiple_of(step * tile, tile), tile)
            result = jnp.dot(inner, downw[:, cols], preferred_element_type=f32).astype(bf16)
            part[s, blocks, :, cols] = result.reshape(count, span, tile)
            size = jnp.abs(result.astype(f32))
            for k in range(tile // 128):
                top = jnp.maximum(top, size[:, k * 128 : (k + 1) * 128])
            return top

        top = lax.fori_loop(0, width // tile, take_down, jnp.zeros((count * span, 128), f32))
        top = jnp.max(top, axis=1, keepdims=True)
        lane_group = lax.div(lax.broadcasted_iota(i32, (SUB, 128), 1), group)
        for k in range(count):
            spread = jnp.zeros((SUB, 128), f32)
            for i in range(nx):
                start = k * span + i * SUB
                spread = jnp.where(lane_group == i, top[start : start + SUB], spread)
            bound[s, first + k] = spread

    def both(s):
        return (lax.rem(mz + nz - s, nz), lax.rem(mz + s, nz))

    @pl.loop(1, half - 1)
    def _(s):
        for i in seq:
            for d in range(2):
                out_copy(s - 1, d, i).wait_recv()
                out_copy(s, d, i).start()
        compute(s, 0, both(s))

    for i in seq:
        for d in range(2):
            out_copy(half - 2, d, i).wait_recv()
            far_copy(d, i).start()
    compute(half - 1, 0, both(half - 1))

    def level_copy(k, to, d):
        return remote(level_out.at[k, d], level_in.at[to, d], lv_send.at[k, d], lv_recv.at[to, d], back_way[d])

    def bound_in(k, d):
        return TOP_CODE * jnp.exp(level_in[k, d].astype(i32).astype(f32) * (1.0 / LEVELS))

    def send_level(k, to, d, most):
        level = jnp.ceil(jnp.log(jnp.maximum(most, 1e-30) * (1.0 / TOP_CODE)) * LEVELS)
        level_out[k, d] = level.astype(i32).astype(i16)
        level_copy(k, to, d).start()

    def level_of(ref, k, d, i):
        return ref[k, d].astype(i32).astype(f32)[:, i * group : i * group + 1]

    def write(ref, i, side, value, k, d):
        codes = jnp.round(value * jnp.exp(level_of(level_out, k, d, i) * (-1.0 / LEVELS)))
        ref[sub(i), sides[side]] = codes.astype(i32).astype(i16)

    def read(ref, i, side, k, d):
        codes = ref[sub(i), sides[side]].astype(i32).astype(f32)
        return codes * jnp.exp(level_of(level_in, k, d, i) * (1.0 / LEVELS))

    def term(s, d, i, side):
        return part[s, d, sub(i), sides[side]].astype(f32)

    def back_copy(s, d, i):
        src, dst = rs.at[s, d, sub(i)], rs.at[s - 1, d, sub(i)]
        return remote(src, dst, rs_send.at[s], rs_recv.at[s - 1, d, i], back_way[d])

    def half_copy(d, i, side):
        src, dst = rs.at[half - 1, d, sub(i), sides[side]], rs.at[half - 2, d, sub(i), sides[side]]
        return remote(src, dst, rs_send.at[half - 1], rs_recv.at[half - 2, d, i], back_way[d])

    def first_copy(d, i):
        src, dst = stage.at[sub(i), sides[d]], rs.at[half - 1, d, sub(i), sides[d]]
        return remote(src, dst, rs_send.at[0], rs_recv.at[half - 1, d, i], back_way[d])

    def last_copy(d, i, side):
        src, dst = rs.at[1, d, sub(i), sides[side]], rs.at[0, d, sub(i), sides[side]]
        return remote(src, dst, rs_send.at[1], last_recv.at[d, i, side], back_way[d])

    for d in range(2):
        send_level(half, half, d, bound[half - 1, d])
    for i in back_seq:
        for d in range(2):
            write(rs.at[half - 1, d], i, 1 - d, term(half - 1, d, i, 1 - d), half, d)
            half_copy(d, i, 1 - d).start()
    for i in seq:
        for d in range(2):
            far_copy(d, i).wait_recv()
    compute(0, 1, (lax.rem(mz + half, nz),))
    for d in range(2):
        send_level(0, half - 1, d, bound[0, 1])
    for i in back_seq:
        for d in range(2):
            write(stage, i, d, term(0, 1, i, d), 0, d)
            first_copy(d, i).start()
    compute(0, 0, (mz,))
    for d in range(2):
        level_copy(0, half - 1, d).wait_recv()
        send_level(half - 1, half - 2, d, bound_in(half - 1, d) + bound[half - 1, d])
    for i in back_seq:
        for d in range(2):
            first_copy(d, i).wait_recv()
            ref = rs.at[half - 1, d]
            write(ref, i, d, read(ref, i, d, half - 1, d) + term(half - 1, d, i, d), half - 1, d)
            half_copy(d, i, d).start()

    def settle(s):
        remote(ag.at[s], ag.at[s], ag_send.at[s + 1], ag_recv.at[s, 0, 0], right).wait_send()

    for d in range(2):
        level_copy(half, half, d).wait_recv()
        level_copy(half - 1, half - 2, d).wait_recv()
        most = jnp.maximum(bound_in(half, d), bound_in(half - 2, d))
        send_level(half - 2, half - 3, d, most + bound[half - 2, d])
    for i in back_seq:
        for d in range(2):
            back_copy(half - 1, d, i).wait_recv()
            ref = rs.at[half - 2, d]
            for side in range(2):
                level = half - 2 if side == d else half
                write(ref, i, side, read(ref, i, side, level, d) + term(half - 2, d, i, side), half - 2, d)
            back_copy(half - 2, d, i).start()
    settle(half - 2)

    @pl.loop(1, half - 3)
    def _(step):
        s = half - 2 - step
        for d in range(2):
            level_copy(s + 1, s, d).wait_recv()
            send_level(s, s - 1, d, bound_in(s, d) + bound[s, d])
        for i in back_seq:
            for d in range(2):
                back_copy(s + 1, d, i).wait_recv()
                ref = rs.at[s, d]
                for side in range(2):
                    write(ref, i, side, read(ref, i, side, s, d) + term(s, d, i, side), s, d)
                back_copy(s, d, i).start()
        settle(s)

    for d in range(2):
        level_copy(2, 1, d).wait_recv()
        send_level(1, 0, d, bound_in(1, d) + bound[1, d])
    for i in back_seq:
        for d in range(2):
            back_copy(2, d, i).wait_recv()
        for side in range(2):
            for d in range(2):
                ref = rs.at[1, d]
                write(ref, i, side, read(ref, i, side, 1, d) + term(1, d, i, side), 1, d)
                last_copy(d, i, side).start()
    settle(1)

    for i in range(1, nx):
        gate_copy(i).wait_recv()

    def y_copy(h, i, side):
        device = ((sec_up, sec_down)[h], columns[i] * nz + mz)
        cols = pl.ds(side * quarter, quarter)
        src, dst = ysend.at[h, sub(i), cols], yrecv.at[h, sub_at(mx), cols]
        return remote(src, dst, y_send.at[h], y_recv.at[h, mx], device)

    for i in range(1, nx):
        for side in range(4):
            row_copy(i, side).wait_send()
        gate_copy(i).wait_send()
    for d in range(2):
        remote(ag.at[0, 0], ag.at[1, d], ag_send.at[d], ag_recv.at[1, d, 0], right).wait_send()
        far = ag.at[half - 1, d, :, sides[d]]
        remote(far, far, ag_send.at[half + d], ag_recv.at[0, 1, 0], right).wait_send()
    remote(stage, rs.at[0, 0], rs_send.at[0], rs_recv.at[0, 0, 0], right).wait_send()
    for s in range(2, half):
        remote(rs.at[s], rs.at[s - 1], rs_send.at[s], rs_recv.at[0, 0, 0], right).wait_send()
    for d in range(2):
        level_copy(1, 0, d).wait()
        for k in (0, *range(2, half + 1)):
            level_copy(k, 0, d).wait_send()
    for copy in near_copies:
        copy.wait()

    for i in back_seq:
        gate = gown[sub(i), 0:1]
        for side in range(2):
            for d in range(2):
                last_copy(d, i, side).wait_recv()
            total = term(0, 0, i, side)
            for d in range(2):
                total = total + read(rs.at[0, d], i, side, 0, d)
            value = ag[0, 0, sub(i), sides[side]].astype(f32) + gate * total
            for h in range(2):
                picked = value[h * CAP : (h + 1) * CAP]
                folded = jnp.concatenate([picked[:, :quarter], picked[:, quarter:]], axis=0)
                ysend[h, sub(i), pl.ds(side * quarter, quarter)] = folded.astype(bf16)
                y_copy(h, i, side).start()

    for h in range(2):
        for e in range(nx):
            remote(ysend.at[h, sub(e)], yrecv.at[h, sub(e)], y_send.at[h], y_recv.at[h, e], next_of[h]).wait_recv()

    for d in range(2):
        remote(ysend.at[d], yrecv.at[d], y_send.at[d], y_recv.at[d, 0], right).wait_send()
    remote(rs.at[1], rs.at[0], rs_send.at[1], rs_recv.at[0, 0, 0], right).wait_send()


def place_rows(near, places, moved, outf, outb, done, out_sem):
    width = near.shape[2]
    fold = width // 2
    span = moved.shape[1]
    stores = []
    quarter = fold // 2
    for h in range(2):
        place = places[h]
        with_share = jnp.max(place.astype(f32), axis=1, keepdims=True) > 0.5
        for side in range(2):
            share = moved[h, :, side * quarter : (side + 1) * quarter]
            for k in range(2):
                cols = pl.ds((2 * side + k) * quarter, quarter)
                spots = place[:, k * span : (k + 1) * span]
                here = jnp.dot(spots, share, preferred_element_type=f32)
                done[h, :, cols] = jnp.where(with_share, here, near[h, :, cols].astype(f32)).astype(bf16)
                store = pltpu.make_async_copy(done.at[h, :, cols], (outf, outb)[h].at[:, cols], out_sem.at[h, 2 * side + k])
                store.start()
                stores.append(store)
    for store in stores:
        store.wait()


def per_device(x_fwd, ids_fwd, gates_fwd, dy_bwd, ids_bwd, gates_bwd, saved_hidden, w_up, w_down):
    nsec = lax.axis_size("section")
    devices = lax.axis_size("expert")
    hid = w_up.shape[2]
    nz = FF // hid
    nx = devices // nz
    half = nz // 2
    tokens, width = x_fwd.shape[1:]
    span = SUB * nx
    choices = ids_fwd.shape[2]
    any_space = pl.BlockSpec(memory_space=pl.ANY)
    vmem = pl.BlockSpec(memory_space=pltpu.VMEM)
    dma = pltpu.SemaphoreType.DMA
    near, near_plr, yrecv = pl.pallas_call(
        functools.partial(kernel, nsec, nx, nz),
        out_shape=[
            pltpu.VMEM((2, tokens, width), bf16),
            pltpu.VMEM((2, tokens, 2 * span), bf16),
            pltpu.VMEM((2, span, width // 2), bf16),
        ],
        in_specs=[any_space] * 9,
        out_specs=[vmem] * 3,
        scratch_shapes=[
            pltpu.VMEM((half + 1, 2, SUB, 128), i16),
            pltpu.VMEM((half + 1, 2, SUB, 128), i16),
            pltpu.VMEM((half, 2, SUB, 128), f32),
            pltpu.VMEM((2, tokens, width), bf16),
            pltpu.VMEM((2, choices, tokens), i32),
            pltpu.VMEM((2, choices, tokens), f32),
            pltpu.VMEM((span, width), bf16),
            pltpu.VMEM((span, 128), f32),
            pltpu.VMEM((span, 128), f32),
            pltpu.VMEM((width, 2 * hid), bf16),
            pltpu.VMEM((2 * hid, width), bf16),
            pltpu.VMEM((nx, nz, CAP, hid), f32),
            pltpu.VMEM((half, 2, span, width), bf16),
            pltpu.VMEM((half, 2, span, width), i16),
            pltpu.VMEM((span, width), i16),
            pltpu.VMEM((half, 2, span, width), bf16),
            pltpu.VMEM((2, tokens, 2 * span), bf16),
            pltpu.VMEM((2, span, width // 2), bf16),
            dma((9,)),
            dma((nx - 1, 4)), dma((nx - 1, 4)), dma((nx - 1,)), dma((nx - 1,)),
            dma((half + 2,)), dma((half, 2, nx)),
            dma((half,)), dma((half, 2, nx)),
            dma((2, 2)), dma((2, 2)), dma((2,)), dma((2, nx)), dma((2, nx, 2)), dma((half + 1, 2)), dma((half + 1, 2)),
        ],
        compiler_params=pltpu.CompilerParams(
            collective_id=0, has_side_effects=True, vmem_limit_bytes=56 * 1024 * 1024
        ),
    )(
        x_fwd[0], dy_bwd[0], ids_fwd[0].T, gates_fwd[0].T, ids_bwd[0].T, gates_bwd[0].T,
        saved_hidden[0].reshape(nx, nz, CAP, hid), w_up[0], w_down[0],
    )
    outs = pl.pallas_call(
        place_rows,
        out_shape=[jax.ShapeDtypeStruct((tokens, width), bf16)] * 2,
        in_specs=[vmem] * 3,
        out_specs=[any_space] * 2,
        scratch_shapes=[pltpu.VMEM((2, tokens, width), bf16), dma((2, 4))],
        compiler_params=pltpu.CompilerParams(vmem_limit_bytes=32 * 1024 * 1024),
    )(*(pltpu.with_memory_space_constraint(v, pltpu.VMEM) for v in (near, near_plr, yrecv)))
    return (outs[0][None], outs[1][None])


def solution(mesh):
    in_specs = (
        P("section", "expert", None),
        P("section", "expert", None),
        P("section", "expert", None),
        P("section", "expert", None),
        P("section", "expert", None),
        P("section", "expert", None),
        P("section", None, "expert"),
        P("section", None, "expert"),
        P("section", "expert", None),
    )
    out_specs = (P("section", "expert", None), P("section", "expert", None))
    return jax.shard_map(
        per_device, mesh=mesh, in_specs=in_specs, out_specs=out_specs, check_vma=False
    )
```
